256 devices in a mesh: dp: 16 (over y, x), ctx: 16 (over z, core).
Axes of the slice: x: 4, y: 4, z: 8, core: 2. Of those that a mesh axis runs over, the one named last changes fastest.
Arguments:
- hidden_in: bfloat16 [16, 3072, 16384], P('dp', 'ctx'), may hold values from -8 to 8
- queries: bfloat16 [16, 3072, 1024], P('dp', 'ctx'), may hold values from -14 to 14
- grad_out: bfloat16 [16, 3072, 1024], P('dp', 'ctx'), may hold values from -6 to 6
- w_key: bfloat16 [16384, 128], P('dp'), may hold values from -1 to 1
- w_value: bfloat16 [16384, 128], P('dp'), may hold values from -0.046875 to 0.046875
- stretch_order: int32 [32], replicated, may hold values from 0 to 31, each once
- doc_lengths: int32 [16, 8], P('dp'), may hold values from 1 to 1536, 3072 in all within a row
Outputs:
- query_grad: bfloat16 [16, 3072, 1024], P('dp', 'ctx')
- key_weight_grad: float32 [16384, 128], P('dp')
- value_weight_grad: float32 [16384, 128], P('dp')
The draws below stay inside these ranges and needn't reach their ends.
Inputs may be any that keep to these rules, and one draw needn't show every extreme that they name: `stretch_order`: every block number appears exactly once. `doc_lengths`: each sequence's lengths sum to 3072, and one of them is 1536.
All inputs are finite; a program needn't handle non-finite values.
Results may differ from the reference program's by a relative error of at most 0.03.
Values may be sent and summed in bfloat16 or wider, within the bound.
A program may use at most 128 MiB of HBM per device.

```python
import math
import jax
import jax.numpy as jnp
import numpy as np
from jax import lax

D = 16384
HEADS = 8
HD = 128
TOK_DEV = 192
DOCS = 8
SEQ = 3072
SEQS = 16
STRETCHES = 32


def draw_hidden_in(key, part):
    key = jax.random.fold_in(key, 11)
    base = jnp.clip(jax.random.normal(key, (SEQS, SEQ, D), jnp.float32), -6.0, 6.0)
    return base.astype(jnp.bfloat16)


def draw_w_key(key, part):
    key = jax.random.fold_in(key, 12)
    base = jnp.clip(jax.random.normal(key, (D, HD), jnp.float32), -6.0, 6.0) * D ** (-0.5)
    return base.astype(jnp.bfloat16)


def draw_queries(key, part):
    key = jax.random.fold_in(key, 13)
    base = jnp.clip(jax.random.normal(key, (SEQS, SEQ, HEADS, HD), jnp.float32), -6.0, 6.0)
    return base.reshape(SEQS, SEQ, HEADS * HD).astype(jnp.bfloat16)


def block_levels(own_key, extent, pieces, least, largest):
    gain, own = 1.0, jax.random.fold_in(own_key, 6)
    for axis_at, shards_of in pieces:
        draws = jnp.exp(jax.random.uniform(jax.random.fold_in(own, axis_at), (shards_of,), jnp.float32, least / len(pieces), largest / len(pieces)))
        gain = gain * jnp.repeat(draws, extent[axis_at] // shards_of).reshape([-1 if axis == axis_at else 1 for axis in range(len(extent))])
    return gain


def split_up(count, total, bound, skew):
    loads = [(1 << 20) // math.isqrt(rank ** skew) + 1 for rank in range(2, count + 1)]
    surplus, holding = total - bound - (count - 1), [1] * (count - 1)
    while surplus > 0:
        movable = [i for i in range(count - 1) if holding[i] < bound]
        whole, budget = sum([loads[i] for i in movable]), surplus
        for i in movable:
            extra = min(bound - holding[i], max(1, budget * loads[i] // whole), surplus)
            holding[i] = holding[i] + extra
            surplus = surplus - extra
    return np.array([bound] + holding)


def uneven(own_key, amount, total, bound, slope):
    if amount == 2:
        one = jax.random.randint(own_key, (), max(1, total - bound), min(bound, total - 1) + 1)
        return jnp.stack([one, total - one])
    sizes = jnp.asarray(split_up(amount, total, bound, slope), jnp.int32)
    couples = (amount - 1) // 2
    donor, taker = sizes[1:1 + 2 * couples:2], sizes[2:2 + 2 * couples:2]
    margin = jnp.minimum(donor - 1, bound - taker)
    moved = jax.random.randint(jax.random.fold_in(own_key, 1), (couples,), 0, 1 << 20) % (margin + 1)
    sizes = sizes.at[1:1 + 2 * couples:2].set(donor - moved).at[2:2 + 2 * couples:2].set(taker + moved)
    return sizes[jax.random.permutation(jax.random.fold_in(own_key, 2), amount)]


def normal_values(own_key, shape, width, limit, split=(), kind=jnp.bfloat16):
    array = jax.random.normal(own_key, shape, jnp.float32) * width
    if len(split) > 0:
        array = block_levels(own_key, shape, split, -0.22, 0.18) * array
    return jnp.clip(array, min=-limit, max=limit).astype(kind)


def setup_inputs(seed: int = 0) -> dict:
    keys = jax.random.split(jax.random.key(seed), 8)
    return {
        "hidden_in": draw_hidden_in(jax.random.fold_in(keys[7], 71), 0),
        "queries": draw_queries(jax.random.fold_in(keys[7], 71), 0),
        "grad_out": normal_values(keys[2], (SEQS, SEQ, HEADS * HD), 1.0, 6.0, ((0, 16), (1, 16))),
        "w_key": draw_w_key(jax.random.fold_in(keys[7], 71), 0),
        "w_value": normal_values(keys[4], (D, HD), D ** -0.5, 0.046875, ((0, 16),)),
        "stretch_order": jax.random.permutation(keys[5], STRETCHES).astype(jnp.int32),
        "doc_lengths": jax.vmap(lambda own: uneven(own, DOCS, SEQ, SEQ // 2, 2))(jax.random.split(keys[6], SEQS)).reshape((SEQS, DOCS)).astype(jnp.int32),
    }


def positions(stretch_order, row_count, stretch_rows):
    stored = jnp.arange(row_count, dtype=jnp.int32)
    return stretch_order[stored // stretch_rows] * stretch_rows + stored % stretch_rows

def doc_numbers(place, lengths):
    doc_ends = jnp.cumsum(lengths)
    return lax.optimization_barrier(jnp.sum((place[:, None] >= doc_ends[None, :]).astype(jnp.int32), axis=1))

def attention_grads(query_rows, key_rows, value_rows, cotangent, allowed):
    row_count = query_rows.shape[0]
    score_scale = 1.0 / math.sqrt(HD)
    query_three = query_rows.reshape(row_count, HEADS, HD).astype(jnp.float32)
    cot_three = cotangent.reshape(row_count, HEADS, HD).astype(jnp.float32)
    keys_float = key_rows.astype(jnp.float32)
    values_float = value_rows.astype(jnp.float32)
    scores = jnp.einsum('thd,kd->htk', query_three, keys_float) * score_scale
    masked = jnp.where(allowed[None], scores, -jnp.inf)
    row_max = lax.optimization_barrier(jnp.max(masked, axis=-1, keepdims=True))
    expsum = jnp.where(allowed[None], jnp.exp(masked - row_max), 0.0)
    probabilities = expsum / lax.optimization_barrier(jnp.sum(expsum, axis=-1, keepdims=True))
    probs_low = probabilities.astype(jnp.bfloat16)
    probs_back = probs_low.astype(jnp.float32)
    attended = jnp.einsum('htk,kd->thd', probs_back, values_float)
    delta_rows = lax.optimization_barrier(jnp.sum(cot_three * attended, axis=-1))
    dprob = jnp.einsum('thd,kd->htk', cot_three, values_float)
    dscore = (probabilities * (dprob - jnp.transpose(delta_rows)[:, :, None])).astype(jnp.bfloat16)
    dscore_back = dscore.astype(jnp.float32)
    query_grad = (jnp.einsum('htk,kd->thd', dscore_back, keys_float) * score_scale).astype(jnp.bfloat16)
    key_grad = jnp.einsum('htk,thd->kd', dscore_back, query_three) * score_scale
    value_grad = jnp.einsum('htk,thd->kd', probs_back, cot_three)
    return (query_grad.reshape(row_count, HEADS * HD), jnp.concatenate([key_grad, value_grad], axis=1))

def reference(hidden_in, queries, grad_out, w_key, w_value, stretch_order, doc_lengths):
    stacked = jnp.concatenate([w_key, w_value], axis=1)
    stretch_rows = TOK_DEV // 2
    place = positions(stretch_order, SEQ, stretch_rows)
    causal = place[None, :] <= place[:, None]

    def per_sequence(running, items):
        inputs, query_rows, cotangent, lengths = items
        documents = doc_numbers(place, lengths)
        allowed = causal & (documents[:, None] == documents[None, :])
        projected = jnp.dot(inputs, stacked, preferred_element_type=jnp.float32).astype(jnp.bfloat16)
        query_grad, kv_grads = attention_grads(query_rows, projected[:, :HD], projected[:, HD:], cotangent, allowed)
        kv_low = kv_grads.astype(jnp.bfloat16)
        running = running + jnp.dot(jnp.transpose(inputs), kv_low, preferred_element_type=jnp.float32)
        return (running, query_grad)
    start_sum = jnp.zeros((D, 2 * HD), jnp.float32)
    weight_grads, query_grad = lax.scan(per_sequence, start_sum, (hidden_in, queries, grad_out, doc_lengths))
    return (query_grad, weight_grads[:, :HD], weight_grads[:, HD:])
```

```python
import functools
import math

import jax
import jax.numpy as jnp
from jax import lax
from jax.experimental import pallas as pl
from jax.experimental.pallas import tpu as pltpu
from jax.sharding import PartitionSpec as P

MESH = pl.DeviceIdType.MESH
SIDE = 4
DEPTH = 8
BF = jnp.bfloat16
F32 = jnp.float32
VMEM_LIMIT = 60 * 2**20


def slot_of(x, y):
    return lax.rem(y, SIDE) * SIDE + lax.rem(x, SIDE)


class Place:
    def __init__(self):
        dp, ctx = lax.axis_index("dp"), lax.axis_index("ctx")
        self.dp, self.ctx = dp, ctx
        self.x, self.y = lax.rem(dp, SIDE), lax.div(dp, SIDE)
        self.z, self.core = lax.div(ctx, 2), lax.rem(ctx, 2)

    def partner(self):
        return (self.dp, self.z * 2 + 1 - self.core)

    def along_z(self, d):
        return (self.dp, lax.rem(self.z + d, DEPTH) * 2 + self.core)

    def along(self, axis, d):
        if axis == 0:
            return (slot_of(self.x + d, self.y), self.ctx)
        return (slot_of(self.x, self.y + d), self.ctx)

    def slot(self, half, du, dv):
        if half == 0:
            return slot_of(self.x + du, self.y + dv)
        return slot_of(self.x + dv, self.y + du)


def greet(devices):
    barrier = pltpu.get_barrier_semaphore()
    for device in devices:
        pl.semaphore_signal(barrier, inc=1, device_id=device, device_id_type=MESH)
    pl.semaphore_wait(barrier, len(devices))


class Sender:
    def __init__(self, sems):
        self.sems, self.sent = sems, []

    def __call__(self, src, dst, recv_sem, device):
        copy = pltpu.make_async_remote_copy(
            src_ref=src,
            dst_ref=dst,
            send_sem=self.sems.at[len(self.sent)],
            recv_sem=recv_sem,
            device_id=device,
            device_id_type=MESH,
        )
        copy.start()
        self.sent.append(copy)

    def finish(self):
        for copy in self.sent:
            copy.wait_send()


def arrived(dst, recv_sem, place):
    pltpu.make_async_remote_copy(
        src_ref=dst,
        dst_ref=dst,
        send_sem=recv_sem,
        recv_sem=recv_sem,
        device_id=place.partner(),
        device_id_type=MESH,
    ).wait_recv()


PROJECT_SENDS = 2 * 20 + 1 + 8 + 8


def project_kernel(
    hid_ref, wk_ref, wv_ref, kv_ref, hp_ref,
    hbuf, wbuf, acc, pin, pout,
    own_sem, hs_sem, hr_sem, hp_sem, s_sem, w_sem, p_sem, z_sem, c_sem,
):
    me = Place()
    rows, cols = hid_ref.shape[0], wbuf.shape[2]
    greet(
        [me.partner()]
        + [me.along(a, d) for a in (0, 1) for d in (1, SIDE - 1)]
        + [me.along_z(d) for d in (1, DEPTH - 1)]
    )
    send = Sender(s_sem)

    mine = pl.ds(pl.multiple_of(me.core * cols, cols), cols)
    wbuf[0, me.dp] = wk_ref[mine, :]
    wbuf[1, me.dp] = wv_ref[mine, :]
    half_rows = cols // 2
    parts = (pl.ds(0, half_rows), pl.ds(half_rows, half_rows))
    ahead, back = 1, SIDE - 1

    def w_send(h, slot, axis, d, part=None):
        ref = wbuf.at[h, slot]
        sem = w_sem.at[h, slot, 0 if part is None else part]
        if part is not None:
            ref = ref.at[parts[part]]
        send(ref, ref, sem, me.along(axis, d))

    def w_wait(h, slot, part=None):
        ref = wbuf.at[h, slot]
        if part is not None:
            ref = ref.at[parts[part]]
        arrived(ref, w_sem.at[h, slot, 0 if part is None else part], me)

    for d in (ahead, back):
        for h in (0, 1):
            w_send(h, me.dp, h, d)

    def part_of(s, core):
        return hid_ref.at[:, pl.ds(pl.multiple_of((s * 2 + core) * cols, cols), cols)]

    def h_copies(s):
        own = pltpu.make_async_copy(
            part_of(s, me.core), hbuf.at[s, pl.ds(0, rows)], own_sem.at[s]
        )
        other = pltpu.make_async_remote_copy(
            src_ref=part_of(s, 1 - me.core),
            dst_ref=hbuf.at[s, pl.ds(rows, rows)],
            send_sem=hs_sem.at[s],
            recv_sem=hr_sem.at[s],
            device_id=me.partner(),
            device_id_type=MESH,
        )
        keep = pltpu.make_async_copy(hbuf.at[s, pl.ds(rows, rows)], hp_ref.at[s], hp_sem.at[s])
        return own, other, keep

    @pl.loop(0, SIDE * SIDE)
    def _(i):
        s = slot_of(me.x + lax.rem(i, SIDE), me.y + lax.div(i, SIDE))
        own, other, _ = h_copies(s)
        own.start()
        other.start()

    for d in (ahead, back):
        for h in (0, 1):
            w_send(h, me.dp, 1 - h, d)

    acc[...] = jnp.zeros_like(acc)

    def compute(dx, dy):
        s = slot_of(me.x + dx, me.y + dy)
        own, other, keep = h_copies(s)
        own.wait()
        other.wait_recv()
        keep.start()
        w = jnp.concatenate([wbuf[0, s], wbuf[1, s]], axis=1)
        acc[...] += jnp.dot(hbuf[s], w, preferred_element_type=F32)

    for d, other, part in ((back, ahead, 0), (ahead, back, 1)):
        for h in (0, 1):
            slot = me.slot(h, d, 0)
            w_wait(h, slot)
            w_send(h, slot, h, other, part)
    for d in (back, ahead):
        for h in (0, 1):
            for e in (ahead, back):
                w_send(h, me.slot(h, d, 0), 1 - h, e)
    compute(0, 0)
    for h in (0, 1):
        slot = me.slot(h, 2, 0)
        w_wait(h, slot, 0)
        w_wait(h, slot, 1)
        for e in (ahead, back):
            w_send(h, slot, 1 - h, e)

    def pass_on(du):
        for d, other, part in ((back, ahead, 0), (ahead, back, 1)):
            for h in (0, 1):
                slot = me.slot(h, du, d)
                w_wait(h, slot)
                w_send(h, slot, 1 - h, other, part)

    pass_on(0)

    @pl.loop(0, 4)
    def _(i):
        a, b = lax.div(i, 2), lax.rem(i, 2)
        compute((1 - a) * (1 + 2 * b), a * (1 + 2 * b))

    pass_on(back)
    pass_on(ahead)

    @pl.loop(0, 4)
    def _(i):
        a, b = lax.div(i, 2), lax.rem(i, 2)
        compute(1 + 2 * a, 1 + 2 * b)

    pass_on(2)

    def far(du):
        for h in (0, 1):
            for part in (0, 1):
                w_wait(h, me.slot(h, du, 2), part)

    far(0)

    @pl.loop(0, 2)
    def _(i):
        compute(2 * i, 2 * (1 - i))

    far(back)
    far(ahead)

    @pl.loop(0, 4)
    def _(i):
        a, b = lax.div(i, 2), lax.rem(i, 2)
        compute((1 - a) * 2 + a * (1 + 2 * b), a * 2 + (1 - a) * (1 + 2 * b))

    far(2)
    compute(2, 2)

    pout[...] = acc[rows:, :]
    send(pout, pin, p_sem.at[0], me.partner())
    arrived(pin, p_sem.at[0], me)
    kv_ref[me.ctx] = (acc[:rows, :] + pin[...]).astype(BF)

    def block(d):
        return lax.rem(me.z + d, DEPTH) * 2 + me.core

    half = rows // 2
    z_parts = (pl.ds(0, half), pl.ds(half, half))

    def z_send(d, step, part=None):
        ref = kv_ref.at[block(d)]
        sem = z_sem.at[block(d), 0 if part is None else part]
        if part is not None:
            ref = ref.at[z_parts[part]]
        send(ref, ref, sem, me.along_z(step))

    def z_wait(d, part=None):
        ref = kv_ref.at[block(d)]
        sem = z_sem.at[block(d), 0 if part is None else part]
        if part is not None:
            ref = ref.at[z_parts[part]]
        arrived(ref, sem, me)

    def share(d):
        ref = kv_ref.at[block(d)]
        send(ref, ref, c_sem.at[block(d)], me.partner())

    up, down = 1, DEPTH - 1
    z_send(0, up)
    z_send(0, down)
    share(0)
    for k in (1, 2, 3):
        z_wait(DEPTH - k)
        z_send(DEPTH - k, up, 0 if k == 3 else None)
        z_wait(k)
        z_send(k, down, 1 if k == 3 else None)
        share(DEPTH - k)
        share(k)
    z_wait(4, 0)
    z_wait(4, 1)
    share(4)

    @pl.loop(0, DEPTH)
    def _(i):
        other = i * 2 + 1 - me.core
        arrived(kv_ref.at[other], c_sem.at[other], me)

    @pl.loop(0, SIDE * SIDE)
    def _(s):
        _, other, keep = h_copies(s)
        other.wait_send()
        keep.wait()

    send.finish()


def project(hidden, w_key, w_value):
    rows, width = hidden.shape
    n = SIDE * SIDE
    cols = width // n // 2
    hd = w_key.shape[1]
    dma = pltpu.SemaphoreType.DMA
    return pl.pallas_call(
        project_kernel,
        out_shape=(
            jax.ShapeDtypeStruct((2 * DEPTH, rows, 2 * hd), BF),
            jax.ShapeDtypeStruct((n, rows, cols), BF),
        ),
        in_specs=[pl.BlockSpec(memory_space=pl.ANY)] + [pl.BlockSpec(memory_space=pltpu.VMEM)] * 2,
        out_specs=(pl.BlockSpec(memory_space=pltpu.VMEM), pl.BlockSpec(memory_space=pl.ANY)),
        scratch_shapes=[
            pltpu.VMEM((n, 2 * rows, cols), BF),
            pltpu.VMEM((2, n, cols, hd), BF),
            pltpu.VMEM((2 * rows, 2 * hd), F32),
            pltpu.VMEM((rows, 2 * hd), F32),
            pltpu.VMEM((rows, 2 * hd), F32),
            dma((n,)),
            dma((n,)),
            dma((n,)),
            dma((n,)),
            dma((PROJECT_SENDS,)),
            dma((2, n, 2)),
            dma((1,)),
            dma((2 * DEPTH, 2)),
            dma((2 * DEPTH,)),
        ],
        compiler_params=pltpu.CompilerParams(
            collective_id=0, has_side_effects=True, vmem_limit_bytes=VMEM_LIMIT
        ),
        name="project",
    )(hidden, w_key, w_value)


STRETCH = 96
SPAN = 17
CHUNKS = 6


def attend_kernel(
    order_ref, lens_ref, ctx_ref, kv_ref, q_ref, g_ref, dq_ref, part_ref,
    kp, acc, qs, gs, scores, dprobs,
):
    heads, hd = q_ref.shape[1] // 128, 128
    n_stretch = kv_ref.shape[0] // STRETCH
    factor = math.log2(math.e) / math.sqrt(hd)
    scale = 1.0 / math.sqrt(hd)
    width = heads * STRETCH
    chunk = SPAN * STRETCH // CHUNKS

    @pl.loop(0, n_stretch)
    def _(b):
        src = pl.ds(pl.multiple_of(b * STRETCH, STRETCH), STRETCH)
        dst = pl.ds(pl.multiple_of(order_ref[b] * STRETCH, STRETCH), STRETCH)
        kp[dst, :] = kv_ref[src, :]
        acc[src, :] = jnp.zeros((STRETCH, 2 * hd), F32)

    for t in range(2):
        place = order_ref[ctx_ref[0] * 2 + t]
        first = jnp.maximum(place - (SPAN - 1), 0) * STRETCH
        for h in range(heads):
            at = (slice(t * STRETCH, (t + 1) * STRETCH), slice(h * hd, (h + 1) * hd))
            to = slice(h * STRETCH, (h + 1) * STRETCH)
            qs[to, :] = q_ref[at]
            gs[to, :] = g_ref[at]
        lane = lax.broadcasted_iota(jnp.int32, (1, width), 1)
        spot = place * STRETCH + lax.rem(lane, STRETCH)
        low = jnp.zeros_like(spot)
        end = jnp.int32(0)
        for d in range(lens_ref.shape[0]):
            end = end + lens_ref[d]
            low = jnp.where(spot >= end, end, low)

        def rows_of(c):
            return pl.ds(pl.multiple_of(first + c * chunk, 16), chunk)

        def local(c):
            return pl.ds(pl.multiple_of(c * chunk, 16), chunk)

        def score(c, top):
            k, v = kp[rows_of(c), :hd], kp[rows_of(c), hd:]
            nt = (((1,), (1,)), ((), ()))
            s = lax.dot_general(k, qs[...], nt, preferred_element_type=F32)
            at = first + c * chunk + lax.broadcasted_iota(jnp.int32, (chunk, width), 0)
            s = jnp.where((at >= low) & (at <= spot), s, -1e30)
            scores[local(c), :] = s
            dprobs[local(c), :] = lax.dot_general(v, gs[...], nt, preferred_element_type=F32)
            return jnp.maximum(top, jnp.max(s, axis=0, keepdims=True))

        top = lax.fori_loop(0, CHUNKS, score, jnp.full((1, width), -1e30, F32))

        def weigh(c, sums):
            total, mixed = sums
            e = jnp.exp2((scores[local(c), :] - top) * factor)
            scores[local(c), :] = e
            total = total + jnp.sum(e, axis=0, keepdims=True)
            mixed = mixed + jnp.sum(e * dprobs[local(c), :], axis=0, keepdims=True)
            return total, mixed

        zero = jnp.zeros((1, width), F32)
        total, mixed = lax.fori_loop(0, CHUNKS, weigh, (zero, zero))
        inverse = 1.0 / total
        delta = mixed * inverse

        def grads(c, dqt):
            p = scores[local(c), :] * inverse
            ds = (p * (dprobs[local(c), :] - delta)).astype(BF)
            k = kp[rows_of(c), :hd]
            acc[rows_of(c), :hd] += jnp.dot(ds, qs[...], preferred_element_type=F32)
            acc[rows_of(c), hd:] += jnp.dot(p.astype(BF), gs[...], preferred_element_type=F32)
            return dqt + lax.dot_general(
                k, ds, (((0,), (0,)), ((), ())), preferred_element_type=F32
            )

        dqt = lax.fori_loop(0, CHUNKS, grads, jnp.zeros((hd, width), F32))
        dq = (jnp.transpose(dqt) * scale).astype(BF)
        for h in range(heads):
            dq_ref[t * STRETCH : (t + 1) * STRETCH, h * hd : (h + 1) * hd] = dq[
                h * STRETCH : (h + 1) * STRETCH
            ]

    @pl.loop(0, n_stretch)
    def _(b):
        dst = pl.ds(pl.multiple_of(b * STRETCH, STRETCH), STRETCH)
        src = pl.ds(pl.multiple_of(order_ref[b] * STRETCH, STRETCH), STRETCH)
        part_ref[dst, :hd] = (acc[src, :hd] * scale).astype(BF)
        part_ref[dst, hd:] = acc[src, hd:].astype(BF)


def attend(order, lens, ctx, kv, queries, grad_out):
    seq, width = kv.shape
    span = SPAN * STRETCH
    heads = queries.shape[1] // 128
    smem = pl.BlockSpec(memory_space=pltpu.SMEM)
    vmem = pl.BlockSpec(memory_space=pltpu.VMEM)
    return pl.pallas_call(
        attend_kernel,
        out_shape=(
            jax.ShapeDtypeStruct(queries.shape, BF),
            jax.ShapeDtypeStruct(kv.shape, BF),
        ),
        in_specs=[smem] * 3 + [vmem] * 3,
        out_specs=(vmem, vmem),
        scratch_shapes=[
            pltpu.VMEM((seq, width), BF),
            pltpu.VMEM((seq, width), F32),
            pltpu.VMEM((heads * STRETCH, 128), BF),
            pltpu.VMEM((heads * STRETCH, 128), BF),
            pltpu.VMEM((span, heads * STRETCH), F32),
            pltpu.VMEM((span, heads * STRETCH), F32),
        ],
        compiler_params=pltpu.CompilerParams(vmem_limit_bytes=VMEM_LIMIT),
        name="attend",
    )(order, lens, ctx, kv, queries, grad_out)


WEIGHT_SENDS = 8 + 8 + 1 + 32 + 8 + 7 + 7 + 1


def weight_kernel(
    part_ref, hid_ref, hp_ref, out_ref,
    hbuf, tb, rbuf, zin, zout, gbuf, gt, pr0, pr1, qr0, qr1, fin, zr,
    own_sem, hp_sem, s_sem, d1_sem, d2_sem, d3_sem, p0_sem, p1_sem, q0_sem, q1_sem, f_sem, g_sem, c_sem,
):
    me = Place()
    rows, cols = gbuf.shape[1], hbuf.shape[2]
    n = SIDE * SIDE

    def h_copies(s):
        src = hid_ref.at[:, pl.ds(pl.multiple_of((s * 2 + me.core) * cols, cols), cols)]
        own = pltpu.make_async_copy(src, hbuf.at[s, pl.ds(0, rows)], own_sem.at[s])
        other = pltpu.make_async_copy(hp_ref.at[s], hbuf.at[s, pl.ds(rows, rows)], hp_sem.at[s])
        return own, other

    @pl.loop(0, n)
    def _(s):
        own, other = h_copies(s)
        own.start()
        other.start()

    greet(
        [me.partner()]
        + [me.along(a, d) for a in (0, 1) for d in (1, SIDE - 1)]
        + [me.along_z(d) for d in range(1, DEPTH)]
    )
    send = Sender(s_sem)

    for d in (4, 3, 5, 2, 6, 1, 7, 0):
        to = lax.rem(me.z + d, DEPTH)
        send(part_ref.at[to * 2 + 1 - me.core], rbuf.at[d], d1_sem.at[d], me.partner())

    def own_sum(d):
        arrived(rbuf.at[d], d1_sem.at[d], me)
        to = lax.rem(me.z + d, DEPTH)
        return part_ref[to * 2 + me.core].astype(F32) + rbuf[d].astype(F32)

    half = rows // 2
    z_parts = (pl.ds(0, half), pl.ds(half, half))
    steps = (1, DEPTH - 1)
    total = own_sum(4).astype(BF)
    for w in (0, 1):
        zout[w, 0, z_parts[w]] = total[w * half : (w + 1) * half]
        send(zout.at[w, 0, z_parts[w]], zin.at[w, 0, z_parts[w]], d2_sem.at[w, 0], me.along_z(steps[w]))
    for k in (1, 2, 3):
        for w in (0, 1):
            d = (4 - k) if w == 0 else DEPTH - (4 - k)
            total = own_sum(d)
            if k == 1:
                arrived(zin.at[w, 0, z_parts[w]], d2_sem.at[w, 0], me)
                zout[w, k] = total.astype(BF)
                got = zin[w, 0, z_parts[w]].astype(F32)
                zout[w, k, z_parts[w]] = (total[w * half : (w + 1) * half] + got).astype(BF)
            else:
                arrived(zin.at[w, k - 1], d2_sem.at[w, k - 1], me)
                zout[w, k] = (total + zin[w, k - 1].astype(F32)).astype(BF)
            send(zout.at[w, k], zin.at[w, k], d2_sem.at[w, k], me.along_z(steps[w]))
    total = own_sum(0)
    for w in (0, 1):
        arrived(zin.at[w, 3], d2_sem.at[w, 3], me)
        total = total + zin[w, 3].astype(F32)
    gbuf[0] = total.astype(BF)
    send(gbuf.at[0], gbuf.at[1], d3_sem.at[0], me.partner())
    gt[:, :rows] = jnp.transpose(total).astype(BF)

    @pl.loop(0, n)
    def _(s):
        own, other = h_copies(s)
        own.wait()
        other.wait()

    arrived(gbuf.at[1], d3_sem.at[0], me)
    gt[:, rows:] = jnp.transpose(gbuf[1].astype(F32)).astype(BF)

    def terms(dx, dy):
        s = slot_of(me.x + dx, me.y + dy)
        t = jnp.dot(gt[...], hbuf[s], preferred_element_type=F32).astype(BF)
        hd = t.shape[0] // 2
        tb[0, s] = t[:hd]
        tb[1, s] = t[hd:]

    hd = tb.shape[2]
    parts = (pl.ds(0, hd // 2), pl.ds(hd // 2, hd // 2))
    sides = (1, SIDE - 1)
    turn = (2, 1, 3, 0)

    def first_sends(h):
        for dv in turn:
            for w in (0, 1):
                send(tb.at[h, me.slot(h, 2, dv), parts[w]], pr0.at[h, w, dv], p0_sem.at[h, w, dv], me.along(h, sides[w]))

    @pl.loop(0, SIDE)
    def _(i):
        terms(2, i)

    first_sends(0)

    @pl.loop(0, SIDE - 1)
    def _(i):
        terms(i + lax.div(i, 2), 2)

    first_sends(1)

    @pl.loop(0, (SIDE - 1) * (SIDE - 1))
    def _(i):
        a, b = lax.div(i, 3), lax.rem(i, 3)
        terms(a + lax.div(a, 2), b + lax.div(b, 2))

    def add(h, slot, part, got):
        ref = tb.at[h, slot]
        if part is not None:
            ref = ref.at[parts[part]]
        ref[...] = (ref[...].astype(F32) + got.astype(F32)).astype(BF)

    for dv in turn:
        for h in (0, 1):
            for w in (0, 1):
                slot = me.slot(h, sides[w], dv)
                arrived(pr0.at[h, w, dv], p0_sem.at[h, w, dv], me)
                add(h, slot, w, pr0[h, w, dv])
                send(tb.at[h, slot], pr1.at[h, w, dv], p1_sem.at[h, w, dv], me.along(h, sides[w]))

    def collect(h, dv):
        for w in (0, 1):
            arrived(pr1.at[h, w, dv], p1_sem.at[h, w, dv], me)
        add(h, me.slot(h, 0, dv), None, pr1[h, 0, dv].astype(F32) + pr1[h, 1, dv].astype(F32))

    for h in (0, 1):
        collect(h, 2)
        for w in (0, 1):
            send(tb.at[h, me.slot(h, 0, 2), parts[w]], qr0.at[h, w], q0_sem.at[h, w], me.along(1 - h, sides[w]))
    for w in (0, 1):
        for h in (0, 1):
            slot = me.slot(h, 0, sides[w])
            collect(h, sides[w])
            arrived(qr0.at[h, w], q0_sem.at[h, w], me)
            add(h, slot, w, qr0[h, w])
            send(tb.at[h, slot], qr1.at[h, w], q1_sem.at[h, w], me.along(1 - h, sides[w]))
    for h in (0, 1):
        collect(h, 0)
        for w in (0, 1):
            arrived(qr1.at[h, w], q1_sem.at[h, w], me)
        got = qr1[h, 0].astype(F32) + qr1[h, 1].astype(F32)
        fin[h * hd : (h + 1) * hd] = (tb[h, me.dp].astype(F32) + got).astype(BF)

    piece = 2 * hd // DEPTH

    def eighth(d):
        return pl.ds(pl.multiple_of(lax.rem(me.z + d, DEPTH) * piece, piece), piece)

    for d in (4, 3, 5, 2, 6, 1, 7):
        send(fin.at[eighth(d)], zr.at[d], f_sem.at[d], me.along_z(d))
    total = fin[eighth(0)].astype(F32)
    for d in range(1, DEPTH):
        arrived(zr.at[d], f_sem.at[d], me)
        total = total + zr[d].astype(F32)
    out_ref[me.core, eighth(0)] = total.astype(BF)
    for d in (4, 3, 5, 2, 6, 1, 7):
        ref = out_ref.at[me.core, eighth(0)]
        send(ref, ref, g_sem.at[d], me.along_z(d))
    for d in range(1, DEPTH):
        arrived(out_ref.at[me.core, eighth(DEPTH - d)], g_sem.at[d], me)
    send(out_ref.at[me.core], out_ref.at[me.core], c_sem.at[0], me.partner())
    arrived(out_ref.at[1 - me.core], c_sem.at[0], me)
    send.finish()


def weight_grads(part, hidden, hidden_other):
    blocks, rows, width = part.shape
    n, _, cols = hidden_other.shape
    hd = width // 2
    dma = pltpu.SemaphoreType.DMA
    vmem, hbm = pl.BlockSpec(memory_space=pltpu.VMEM), pl.BlockSpec(memory_space=pl.ANY)
    return pl.pallas_call(
        weight_kernel,
        out_shape=jax.ShapeDtypeStruct((2, width, cols), BF),
        in_specs=[vmem, hbm, hbm],
        out_specs=vmem,
        scratch_shapes=[
            pltpu.VMEM((n, 2 * rows, cols), BF),
            pltpu.VMEM((2, n, hd, cols), BF),
            pltpu.VMEM((DEPTH, rows, width), BF),
            pltpu.VMEM((2, 4, rows, width), BF),
            pltpu.VMEM((2, 4, rows, width), BF),
            pltpu.VMEM((2, rows, width), BF),
            pltpu.VMEM((width, 2 * rows), BF),
            pltpu.VMEM((2, 2, SIDE, hd // 2, cols), BF),
            pltpu.VMEM((2, 2, SIDE, hd, cols), BF),
            pltpu.VMEM((2, 2, hd // 2, cols), BF),
            pltpu.VMEM((2, 2, hd, cols), BF),
            pltpu.VMEM((width, cols), BF),
            pltpu.VMEM((DEPTH, width // DEPTH, cols), BF),
            dma((n,)),
            dma((n,)),
            dma((WEIGHT_SENDS,)),
            dma((DEPTH,)),
            dma((2, 4)),
            dma((1,)),
            dma((2, 2, SIDE)),
            dma((2, 2, SIDE)),
            dma((2, 2)),
            dma((2, 2)),
            dma((DEPTH,)),
            dma((DEPTH,)),
            dma((1,)),
        ],
        compiler_params=pltpu.CompilerParams(
            collective_id=1, has_side_effects=True, vmem_limit_bytes=VMEM_LIMIT
        ),
        name="weights",
    )(part, hidden, hidden_other)


def on_device(hidden_in, queries, grad_out, w_key, w_value, stretch_order, doc_lengths):
    hidden = hidden_in[0]
    rows, hd = hidden.shape[0], w_key.shape[1]
    kv, hidden_other = project(hidden, w_key, w_value)
    ctx = lax.axis_index("ctx").astype(jnp.int32).reshape(1)
    query_grad, part = attend(
        stretch_order, doc_lengths[0], ctx, kv.reshape(-1, 2 * hd), queries[0], grad_out[0]
    )
    sums = weight_grads(part.reshape(kv.shape), hidden, hidden_other)

    def finish(t):
        return jnp.transpose(t, (0, 2, 1)).reshape(-1, hd).astype(F32)

    return query_grad[None], finish(sums[:, :hd]), finish(sums[:, hd:])


def solution(mesh):
    return jax.shard_map(
        on_device,
        mesh=mesh,
        in_specs=(
            P("dp", "ctx", None),
            P("dp", "ctx", None),
            P("dp", "ctx", None),
            P("dp", None),
            P("dp", None),
            P(),
            P("dp", None),
        ),
        out_specs=(P("dp", "ctx", None), P("dp", None), P("dp", None)),
        check_vma=False,
    )
```

```python
import functools
import math

import jax
import jax.numpy as jnp
from jax import lax
from jax.experimental import pallas as pl
from jax.experimental.pallas import tpu as pltpu
from jax.sharding import PartitionSpec as P

MESH = pl.DeviceIdType.MESH
SIDE = 4
DEPTH = 8
BF = jnp.bfloat16
F32 = jnp.float32
VMEM_LIMIT = 60 * 2**20


def slot_of(x, y):
    return lax.rem(y, SIDE) * SIDE + lax.rem(x, SIDE)


class Place:
    def __init__(self):
        dp, ctx = lax.axis_index("dp"), lax.axis_index("ctx")
        self.dp, self.ctx = dp, ctx
        self.x, self.y = lax.rem(dp, SIDE), lax.div(dp, SIDE)
        self.z, self.core = lax.div(ctx, 2), lax.rem(ctx, 2)

    def partner(self):
        return (self.dp, self.z * 2 + 1 - self.core)

    def along_z(self, d):
        return (self.dp, lax.rem(self.z + d, DEPTH) * 2 + self.core)

    def along(self, axis, d):
        if axis == 0:
            return (slot_of(self.x + d, self.y), self.ctx)
        return (slot_of(self.x, self.y + d), self.ctx)

    def slot(self, half, du, dv):
        if half == 0:
            return slot_of(self.x + du, self.y + dv)
        return slot_of(self.x + dv, self.y + du)


def greet(devices):
    barrier = pltpu.get_barrier_semaphore()
    for device in devices:
        pl.semaphore_signal(barrier, inc=1, device_id=device, device_id_type=MESH)
    pl.semaphore_wait(barrier, len(devices))


class Sender:
    def __init__(self, sems):
        self.sems, self.sent = sems, []

    def __call__(self, src, dst, recv_sem, device):
        copy = pltpu.make_async_remote_copy(
            src_ref=src,
            dst_ref=dst,
            send_sem=self.sems.at[len(self.sent)],
            recv_sem=recv_sem,
            device_id=device,
            device_id_type=MESH,
        )
        copy.start()
        self.sent.append(copy)

    def finish(self):
        for copy in self.sent:
            copy.wait_send()


def arrived(dst, recv_sem, place):
    pltpu.make_async_remote_copy(
        src_ref=dst,
        dst_ref=dst,
        send_sem=recv_sem,
        recv_sem=recv_sem,
        device_id=place.partner(),
        device_id_type=MESH,
    ).wait_recv()


PROJECT_SENDS = 2 * 20 + 1 + 14 + 8


def project_kernel(
    hid_ref, wk_ref, wv_ref, kv_ref, hp_ref,
    hbuf, wbuf, acc, pin, pout,
    own_sem, hs_sem, hr_sem, hp_sem, s_sem, w_sem, p_sem, z_sem, c_sem,
):
    me = Place()
    rows, cols = hid_ref.shape[0], wbuf.shape[2]
    greet(
        [me.partner()]
        + [me.along(a, d) for a in (0, 1) for d in (1, SIDE - 1)]
        + [me.along_z(d) for d in (1, DEPTH - 1)]
    )
    send = Sender(s_sem)

    mine = pl.ds(pl.multiple_of(me.core * cols, cols), cols)
    wbuf[0, me.dp] = wk_ref[mine, :]
    wbuf[1, me.dp] = wv_ref[mine, :]
    half_rows = cols // 2
    parts = (pl.ds(0, half_rows), pl.ds(half_rows, half_rows))
    ahead, back = 1, SIDE - 1

    def w_send(h, slot, axis, d, part=None):
        ref = wbuf.at[h, slot]
        sem = w_sem.at[h, slot, 0 if part is None else part]
        if part is not None:
            ref = ref.at[parts[part]]
        send(ref, ref, sem, me.along(axis, d))

    def w_wait(h, slot, part=None):
        ref = wbuf.at[h, slot]
        if part is not None:
            ref = ref.at[parts[part]]
        arrived(ref, w_sem.at[h, slot, 0 if part is None else part], me)

    for d in (ahead, back):
        for h in (0, 1):
            w_send(h, me.dp, h, d)

    def part_of(s, core):
        return hid_ref.at[:, pl.ds(pl.multiple_of((s * 2 + core) * cols, cols), cols)]

    def h_copies(s):
        own = pltpu.make_async_copy(
            part_of(s, me.core), hbuf.at[s, pl.ds(0, rows)], own_sem.at[s]
        )
        other = pltpu.make_async_remote_copy(
            src_ref=part_of(s, 1 - me.core),
            dst_ref=hbuf.at[s, pl.ds(rows, rows)],
            send_sem=hs_sem.at[s],
            recv_sem=hr_sem.at[s],
            device_id=me.partner(),
            device_id_type=MESH,
        )
        keep = pltpu.make_async_copy(hbuf.at[s, pl.ds(rows, rows)], hp_ref.at[s], hp_sem.at[s])
        return own, other, keep

    @pl.loop(0, SIDE * SIDE)
    def _(i):
        s = slot_of(me.x + lax.rem(i, SIDE), me.y + lax.div(i, SIDE))
        own, other, _ = h_copies(s)
        own.start()
        other.start()

    for d in (ahead, back):
        for h in (0, 1):
            w_send(h, me.dp, 1 - h, d)

    acc[...] = jnp.zeros_like(acc)

    def compute(dx, dy):
        s = slot_of(me.x + dx, me.y + dy)
        own, other, keep = h_copies(s)
        own.wait()
        other.wait_recv()
        keep.start()
        w = jnp.concatenate([wbuf[0, s], wbuf[1, s]], axis=1)
        acc[...] += jnp.dot(hbuf[s], w, preferred_element_type=F32)

    for d, other, part in ((back, ahead, 0), (ahead, back, 1)):
        for h in (0, 1):
            slot = me.slot(h, d, 0)
            w_wait(h, slot)
            w_send(h, slot, h, other, part)
    for d in (back, ahead):
        for h in (0, 1):
            for e in (ahead, back):
                w_send(h, me.slot(h, d, 0), 1 - h, e)
    compute(0, 0)
    for h in (0, 1):
        slot = me.slot(h, 2, 0)
        w_wait(h, slot, 0)
        w_wait(h, slot, 1)
        for e in (ahead, back):
            w_send(h, slot, 1 - h, e)

    def pass_on(du):
        for d, other, part in ((back, ahead, 0), (ahead, back, 1)):
            for h in (0, 1):
                slot = me.slot(h, du, d)
                w_wait(h, slot)
                w_send(h, slot, 1 - h, other, part)

    pass_on(0)

    @pl.loop(0, 4)
    def _(i):
        a, b = lax.div(i, 2), lax.rem(i, 2)
        compute((1 - a) * (1 + 2 * b), a * (1 + 2 * b))

    pass_on(back)
    pass_on(ahead)

    @pl.loop(0, 4)
    def _(i):
        a, b = lax.div(i, 2), lax.rem(i, 2)
        compute(1 + 2 * a, 1 + 2 * b)

    pass_on(2)

    def far(du):
        for h in (0, 1):
            for part in (0, 1):
                w_wait(h, me.slot(h, du, 2), part)

    far(0)

    @pl.loop(0, 2)
    def _(i):
        compute(2 * i, 2 * (1 - i))

    far(back)
    far(ahead)

    @pl.loop(0, 4)
    def _(i):
        a, b = lax.div(i, 2), lax.rem(i, 2)
        compute((1 - a) * 2 + a * (1 + 2 * b), a * 2 + (1 - a) * (1 + 2 * b))

    far(2)
    compute(2, 2)

    pout[...] = acc[rows:, :]
    send(pout, pin, p_sem.at[0], me.partner())
    arrived(pin, p_sem.at[0], me)
    kv_ref[me.ctx] = (acc[:rows, :] + pin[...]).astype(BF)

    def block(d):
        return lax.rem(me.z + d, DEPTH) * 2 + me.core

    half = rows // 2
    z_parts = (pl.ds(0, half), pl.ds(half, half))

    def z_send(d, step, part):
        ref, sem = kv_ref.at[block(d), z_parts[part]], z_sem.at[block(d), part]
        send(ref, ref, sem, me.along_z(step))

    def z_wait(d, part):
        arrived(kv_ref.at[block(d), z_parts[part]], z_sem.at[block(d), part], me)

    def share(d):
        ref = kv_ref.at[block(d)]
        send(ref, ref, c_sem.at[block(d)], me.partner())

    up, down = 1, DEPTH - 1
    for first in (0, 1):
        z_send(0, up, first)
        z_send(0, down, 1 - first)
    share(0)
    for k in (1, 2, 3):
        for first in (0, 1):
            z_wait(DEPTH - k, first)
            if k < 3 or first == 0:
                z_send(DEPTH - k, up, first)
            z_wait(k, 1 - first)
            if k < 3 or first == 0:
                z_send(k, down, 1 - first)
        share(DEPTH - k)
        share(k)
    z_wait(4, 0)
    z_wait(4, 1)
    share(4)

    @pl.loop(0, DEPTH)
    def _(i):
        other = i * 2 + 1 - me.core
        arrived(kv_ref.at[other], c_sem.at[other], me)

    @pl.loop(0, SIDE * SIDE)
    def _(s):
        _, other, keep = h_copies(s)
        other.wait_send()
        keep.wait()

    send.finish()


def project(hidden, w_key, w_value):
    rows, width = hidden.shape
    n = SIDE * SIDE
    cols = width // n // 2
    hd = w_key.shape[1]
    dma = pltpu.SemaphoreType.DMA
    return pl.pallas_call(
        project_kernel,
        out_shape=(
            jax.ShapeDtypeStruct((2 * DEPTH, rows, 2 * hd), BF),
            jax.ShapeDtypeStruct((n, rows, cols), BF),
        ),
        in_specs=[pl.BlockSpec(memory_space=pl.ANY)] + [pl.BlockSpec(memory_space=pltpu.VMEM)] * 2,
        out_specs=(pl.BlockSpec(memory_space=pltpu.VMEM), pl.BlockSpec(memory_space=pl.ANY)),
        scratch_shapes=[
            pltpu.VMEM((n, 2 * rows, cols), BF),
            pltpu.VMEM((2, n, cols, hd), BF),
            pltpu.VMEM((2 * rows, 2 * hd), F32),
            pltpu.VMEM((rows, 2 * hd), F32),
            pltpu.VMEM((rows, 2 * hd), F32),
            dma((n,)),
            dma((n,)),
            dma((n,)),
            dma((n,)),
            dma((PROJECT_SENDS,)),
            dma((2, n, 2)),
            dma((1,)),
            dma((2 * DEPTH, 2)),
            dma((2 * DEPTH,)),
        ],
        compiler_params=pltpu.CompilerParams(
            collective_id=0, has_side_effects=True, vmem_limit_bytes=VMEM_LIMIT
        ),
        name="project",
    )(hidden, w_key, w_value)


STRETCH = 96
SPAN = 17


def attend_kernel(
    order_ref, lens_ref, ctx_ref, kv_ref, q_ref, g_ref, dq_ref, part_ref,
    kp, acc, qs, gs, scores, dprobs,
):
    heads, hd = q_ref.shape[1] // 128, 128
    n_stretch = kv_ref.shape[0] // STRETCH
    factor = math.log2(math.e) / math.sqrt(hd)
    scale = 1.0 / math.sqrt(hd)
    width = heads * STRETCH

    @pl.loop(0, n_stretch)
    def _(b):
        src = pl.ds(pl.multiple_of(b * STRETCH, STRETCH), STRETCH)
        dst = pl.ds(pl.multiple_of(order_ref[b] * STRETCH, STRETCH), STRETCH)
        kp[dst, :] = kv_ref[src, :]
        acc[src, :] = jnp.zeros((STRETCH, 2 * hd), F32)

    for t in range(2):
        place = order_ref[ctx_ref[0] * 2 + t]
        first = jnp.maximum(place - (SPAN - 1), 0) * STRETCH
        for h in range(heads):
            at = (slice(t * STRETCH, (t + 1) * STRETCH), slice(h * hd, (h + 1) * hd))
            to = slice(h * STRETCH, (h + 1) * STRETCH)
            qs[to, :] = q_ref[at]
            gs[to, :] = g_ref[at]
        lane = lax.broadcasted_iota(jnp.int32, (1, width), 1)
        spot = place * STRETCH + lax.rem(lane, STRETCH)
        low = jnp.zeros_like(spot)
        end = jnp.int32(0)
        for d in range(lens_ref.shape[0]):
            end = end + lens_ref[d]
            low = jnp.where(spot >= end, end, low)

        window = pl.ds(pl.multiple_of(first, STRETCH), SPAN * STRETCH)
        nt = (((1,), (1,)), ((), ()))
        low, high = low - first, spot - first
        at = lax.broadcasted_iota(jnp.int32, (SPAN * STRETCH, width), 0)
        s = lax.dot_general(kp[window, :hd], qs[...], nt, preferred_element_type=F32)
        s = jnp.where((at >= low) & (at <= high), s, -1e30)
        scores[...] = s
        top = jnp.max(s, axis=0, keepdims=True)
        dprobs[...] = lax.dot_general(kp[window, hd:], gs[...], nt, preferred_element_type=F32)
        e = jnp.exp2((scores[...] - top) * factor)
        scores[...] = e
        inverse = 1.0 / jnp.sum(e, axis=0, keepdims=True)
        delta = jnp.sum(e * dprobs[...], axis=0, keepdims=True) * inverse
        p = scores[...] * inverse
        ds = (p * (dprobs[...] - delta)).astype(BF)
        acc[window, :hd] += jnp.dot(ds, qs[...], preferred_element_type=F32)
        acc[window, hd:] += jnp.dot(p.astype(BF), gs[...], preferred_element_type=F32)
        dqt = lax.dot_general(
            kp[window, :hd], ds, (((0,), (0,)), ((), ())), preferred_element_type=F32
        )
        dq = (jnp.transpose(dqt) * scale).astype(BF)
        for h in range(heads):
            dq_ref[t * STRETCH : (t + 1) * STRETCH, h * hd : (h + 1) * hd] = dq[
                h * STRETCH : (h + 1) * STRETCH
            ]

    @pl.loop(0, n_stretch)
    def _(b):
        dst = pl.ds(pl.multiple_of(b * STRETCH, STRETCH), STRETCH)
        src = pl.ds(pl.multiple_of(order_ref[b] * STRETCH, STRETCH), STRETCH)
        part_ref[dst, :hd] = (acc[src, :hd] * scale).astype(BF)
        part_ref[dst, hd:] = acc[src, hd:].astype(BF)


def attend(order, lens, ctx, kv, queries, grad_out):
    seq, width = kv.shape
    span = SPAN * STRETCH
    heads = queries.shape[1] // 128
    smem = pl.BlockSpec(memory_space=pltpu.SMEM)
    vmem = pl.BlockSpec(memory_space=pltpu.VMEM)
    return pl.pallas_call(
        attend_kernel,
        out_shape=(
            jax.ShapeDtypeStruct(queries.shape, BF),
            jax.ShapeDtypeStruct(kv.shape, BF),
        ),
        in_specs=[smem] * 3 + [vmem] * 3,
        out_specs=(vmem, vmem),
        scratch_shapes=[
            pltpu.VMEM((seq, width), BF),
            pltpu.VMEM((seq, width), F32),
            pltpu.VMEM((heads * STRETCH, 128), BF),
            pltpu.VMEM((heads * STRETCH, 128), BF),
            pltpu.VMEM((span, heads * STRETCH), F32),
            pltpu.VMEM((span, heads * STRETCH), F32),
        ],
        compiler_params=pltpu.CompilerParams(vmem_limit_bytes=VMEM_LIMIT),
        name="attend",
    )(order, lens, ctx, kv, queries, grad_out)


WEIGHT_SENDS = 8 + 14 + 2 + 32 + 8 + 14 + 7 + 15 + 7 + 8
FLAT_ROWS = 80


def weight_kernel(
    part_ref, hid_ref, hp_ref, out_ref,
    hbuf, tb, rbuf, zin, zout, gbuf, gt, pr0, pr1, qr0, qr1, cin, zr, xr,
    own_sem, hp_sem, s_sem, d1_sem, d2_sem, d3_sem, p0_sem, p1_sem, q0_sem, q1_sem, n_sem, f_sem, x_sem, g_sem, c_sem,
):
    me = Place()
    rows, cols = gbuf.shape[1], hbuf.shape[2]
    n = SIDE * SIDE

    def h_copies(s):
        src = hid_ref.at[:, pl.ds(pl.multiple_of((s * 2 + me.core) * cols, cols), cols)]
        own = pltpu.make_async_copy(src, hbuf.at[s, pl.ds(0, rows)], own_sem.at[s])
        other = pltpu.make_async_copy(hp_ref.at[s], hbuf.at[s, pl.ds(rows, rows)], hp_sem.at[s])
        return own, other

    @pl.loop(0, n)
    def _(s):
        own, other = h_copies(s)
        own.start()
        other.start()

    greet(
        [me.partner()]
        + [me.along(a, d) for a in (0, 1) for d in (1, SIDE - 1)]
        + [me.along_z(d) for d in (1, DEPTH - 1)]
    )
    send = Sender(s_sem)
    z_steps = (1, DEPTH - 1)

    def z_at(d):
        return lax.rem(me.z + d, DEPTH)

    def target(w, k):
        return 4 - k if w == 0 else DEPTH - 4 + k

    for d in (4, 3, 5, 2, 6, 1, 7, 0):
        send(part_ref.at[z_at(d) * 2 + 1 - me.core], rbuf.at[d], d1_sem.at[d], me.partner())

    half = rows // 2
    pieces = (pl.ds(0, half), pl.ds(half, half))
    known = set()

    def own_sum(d, piece):
        if d not in known:
            known.add(d)
            arrived(rbuf.at[d], d1_sem.at[d], me)
        mine = part_ref[z_at(d) * 2 + me.core, pieces[piece]]
        return mine.astype(F32) + rbuf[d, pieces[piece]].astype(F32)

    def kv_step(w, k, piece, first):
        total = own_sum(target(w, k), piece)
        if not first:
            arrived(zin.at[w, k - 1, pieces[piece]], d2_sem.at[w, k - 1, piece], me)
            total = total + zin[w, k - 1, pieces[piece]].astype(F32)
        ref = zout.at[w, k, pieces[piece]]
        ref[...] = total.astype(BF)
        send(ref, zin.at[w, k, pieces[piece]], d2_sem.at[w, k, piece], me.along_z(z_steps[w]))

    for w in (0, 1):
        kv_step(w, 0, w, True)
    for w in (0, 1):
        kv_step(w, 1, 1 - w, True)
    for k in (1, 2, 3):
        for w in (0, 1):
            kv_step(w, k, w, False)
        if k < 3:
            for w in (0, 1):
                kv_step(w, k + 1, 1 - w, False)
    for piece in (0, 1):
        total = own_sum(0, piece)
        for w in (0, 1):
            arrived(zin.at[w, 3, pieces[piece]], d2_sem.at[w, 3, piece], me)
            total = total + zin[w, 3, pieces[piece]].astype(F32)
        ref = gbuf.at[0, pieces[piece]]
        ref[...] = total.astype(BF)
        send(ref, gbuf.at[1, pieces[piece]], d3_sem.at[piece], me.partner())
    gt[:, :rows] = jnp.transpose(gbuf[0].astype(F32)).astype(BF)

    @pl.loop(0, n)
    def _(s):
        own, other = h_copies(s)
        own.wait()
        other.wait()

    for piece in (0, 1):
        arrived(gbuf.at[1, pieces[piece]], d3_sem.at[piece], me)
    gt[:, rows:] = jnp.transpose(gbuf[1].astype(F32)).astype(BF)

    hd = tb.shape[2]
    groups = DEPTH // 2

    def terms(dx, dy):
        s = slot_of(me.x + dx, me.y + dy)
        t = jnp.dot(gt[...], hbuf[s], preferred_element_type=F32).astype(BF)
        for j in range(DEPTH):
            h, g = divmod(j, groups)
            tb[j, s] = t[h * hd : (h + 1) * hd, g * hd : (g + 1) * hd]

    sides = (1, SIDE - 1)

    def flat(h, slot, dv, w=None):
        cut = 48 if dv % 2 == 0 else 32
        at = pl.ds(0, FLAT_ROWS) if w is None else pl.ds(0, cut) if w == 0 else pl.ds(cut, FLAT_ROWS - cut)
        return tb.at[pl.ds(groups * h, groups), slot, at], at

    def first_sends(h):
        for dv in (2, 1, 3, 0):
            for w in (0, 1):
                ref, at = flat(h, me.slot(h, 2, dv), dv, w)
                send(ref, pr0.at[h, w, dv, :, at], p0_sem.at[h, w, dv], me.along(h, sides[w]))

    @pl.loop(0, SIDE)
    def _(i):
        terms(2, i)

    first_sends(0)

    @pl.loop(0, SIDE - 1)
    def _(i):
        terms(i + lax.div(i, 2), 2)

    first_sends(1)

    @pl.loop(0, (SIDE - 1) * (SIDE - 1))
    def _(i):
        a, b = lax.div(i, 3), lax.rem(i, 3)
        terms(a + lax.div(a, 2), b + lax.div(b, 2))

    def add(ref, *got):
        total = ref[...].astype(F32)
        for g in got:
            total = total + g.astype(F32)
        ref[...] = total.astype(BF)

    deep = pl.ds(FLAT_ROWS, hd - FLAT_ROWS)
    slots = (pl.ds(0, n // 2), pl.ds(n // 2, n // 2))

    def deep_step(k, w, piece, first=False):
        ref = tb.at[z_at(target(w, k)), slots[piece], deep]
        if not first:
            got = cin.at[w, k - 1, slots[piece]]
            arrived(got, n_sem.at[w, k - 1, piece], me)
            add(ref, got[...])
        send(ref, cin.at[w, k, slots[piece]], n_sem.at[w, k, piece], me.along_z(z_steps[w]))

    def second_sends(dv):
        for h in (0, 1):
            for w in (0, 1):
                slot = me.slot(h, sides[w], dv)
                ref, at = flat(h, slot, dv, w)
                got = pr0.at[h, w, dv, :, at]
                arrived(got, p0_sem.at[h, w, dv], me)
                add(ref, got[...])
                send(flat(h, slot, dv)[0], pr1.at[h, w, dv], p1_sem.at[h, w, dv], me.along(h, sides[w]))

    def collect(h, dv):
        for w in (0, 1):
            arrived(pr1.at[h, w, dv], p1_sem.at[h, w, dv], me)
        add(flat(h, me.slot(h, 0, dv), dv)[0], pr1[h, 0, dv], pr1[h, 1, dv])

    def third_sends(h):
        for w in (0, 1):
            ref, at = flat(h, me.slot(h, 0, 2), h, w)
            send(ref, qr0.at[h, w, :, at], q0_sem.at[h, w], me.along(1 - h, sides[w]))

    def fourth_sends(h, w):
        slot = me.slot(h, 0, sides[w])
        ref, at = flat(h, slot, h, w)
        got = qr0.at[h, w, :, at]
        arrived(got, q0_sem.at[h, w], me)
        add(ref, got[...])
        send(flat(h, slot, 0)[0], qr1.at[h, w], q1_sem.at[h, w], me.along(1 - h, sides[w]))

    for w in (0, 1):
        deep_step(0, w, w, True)
    for w in (0, 1):
        deep_step(1, w, 1 - w, True)
    second_sends(2)
    second_sends(1)
    for w in (0, 1):
        deep_step(1, w, w)
    second_sends(3)
    second_sends(0)
    for w in (0, 1):
        deep_step(2, w, 1 - w)
    for h in (0, 1):
        collect(h, 2)
        third_sends(h)
    for w in (0, 1):
        deep_step(2, w, w)
    for w in (0, 1):
        for h in (0, 1):
            collect(h, sides[w])
            fourth_sends(h, w)
    for w in (0, 1):
        deep_step(3, w, 1 - w)
    for h in (0, 1):
        collect(h, 0)
    for w in (0, 1):
        deep_step(3, w, w)
    for h in (0, 1):
        for w in (0, 1):
            arrived(qr1.at[h, w], q1_sem.at[h, w], me)
        add(flat(h, me.dp, 0)[0], qr1[h, 0], qr1[h, 1])
    rows_first = pl.ds(0, FLAT_ROWS)
    for d in (4, 3, 5, 2, 6, 1, 7):
        send(tb.at[z_at(d), me.dp, rows_first], zr.at[d], f_sem.at[d], me.along_z(d))
    for piece in (0, 1):
        ref = tb.at[me.z, slots[piece], deep]
        for w in (0, 1):
            arrived(cin.at[w, 3, slots[piece]], n_sem.at[w, 3, piece], me)
        add(ref, cin[0, 3, slots[piece]], cin[1, 3, slots[piece]])
    for far in range(4, 0, -1):
        for dx in range(SIDE):
            for dy in range(SIDE):
                if min(dx, SIDE - dx) + min(dy, SIDE - dy) == far:
                    slot = slot_of(me.x + dx, me.y + dy)
                    send(tb.at[me.z, slot, deep], xr.at[dy * SIDE + dx], x_sem.at[dy * SIDE + dx], (slot, me.ctx))

    top = tb[me.z, me.dp, rows_first].astype(F32)
    for d in range(1, DEPTH):
        arrived(zr.at[d], f_sem.at[d], me)
        top = top + zr[d].astype(F32)
    low = tb[me.z, me.dp, deep].astype(F32)
    for i in range(1, n):
        arrived(xr.at[i], x_sem.at[i], me)
        low = low + xr[i].astype(F32)
    done = jnp.transpose(jnp.concatenate([top, low], axis=0)).astype(BF)

    def block(d, core):
        j = z_at(d)
        at = core * cols + lax.rem(j, groups) * hd
        return out_ref.at[lax.div(j, groups), pl.ds(pl.multiple_of(at, hd), hd)]

    def share(d):
        send(block(d, me.core), block(d, me.core), c_sem.at[d], me.partner())

    block(0, me.core)[...] = done
    for d in (4, 3, 5, 2, 6, 1, 7):
        send(block(0, me.core), block(0, me.core), g_sem.at[d], me.along_z(d))
    share(0)
    for d in (1, 7, 2, 6, 3, 5, 4):
        arrived(block(d, me.core), g_sem.at[DEPTH - d], me)
        share(d)
    for d in range(DEPTH):
        arrived(block(d, 1 - me.core), c_sem.at[d], me)
    send.finish()


def weight_grads(part, hidden, hidden_other):
    blocks, rows, width = part.shape
    n, _, cols = hidden_other.shape
    hd = width // 2
    dma = pltpu.SemaphoreType.DMA
    groups = DEPTH // 2
    vmem, hbm = pl.BlockSpec(memory_space=pltpu.VMEM), pl.BlockSpec(memory_space=pl.ANY)
    return pl.pallas_call(
        weight_kernel,
        out_shape=jax.ShapeDtypeStruct((2, 2 * cols, hd), BF),
        in_specs=[vmem, hbm, hbm],
        out_specs=vmem,
        scratch_shapes=[
            pltpu.VMEM((n, 2 * rows, cols), BF),
            pltpu.VMEM((DEPTH, n, hd, hd), BF),
            pltpu.VMEM((DEPTH, rows, width), BF),
            pltpu.VMEM((2, 4, rows, width), BF),
            pltpu.VMEM((2, 4, rows, width), BF),
            pltpu.VMEM((2, rows, width), BF),
            pltpu.VMEM((width, 2 * rows), BF),
            pltpu.VMEM((2, 2, SIDE, groups, FLAT_ROWS, hd), BF),
            pltpu.VMEM((2, 2, SIDE, groups, FLAT_ROWS, hd), BF),
            pltpu.VMEM((2, 2, groups, FLAT_ROWS, hd), BF),
            pltpu.VMEM((2, 2, groups, FLAT_ROWS, hd), BF),
            pltpu.VMEM((2, 4, n, hd - FLAT_ROWS, hd), BF),
            pltpu.VMEM((DEPTH, FLAT_ROWS, hd), BF),
            pltpu.VMEM((n, hd - FLAT_ROWS, hd), BF),
            dma((n,)),
            dma((n,)),
            dma((WEIGHT_SENDS,)),
            dma((DEPTH,)),
            dma((2, 4, 2)),
            dma((2,)),
            dma((2, 2, SIDE)),
            dma((2, 2, SIDE)),
            dma((2, 2)),
            dma((2, 2)),
            dma((2, 4, 2)),
            dma((DEPTH,)),
            dma((n,)),
            dma((DEPTH,)),
            dma((DEPTH,)),
        ],
        compiler_params=pltpu.CompilerParams(
            collective_id=1, has_side_effects=True, vmem_limit_bytes=VMEM_LIMIT
        ),
        name="weights",
    )(part, hidden, hidden_other)


def on_device(hidden_in, queries, grad_out, w_key, w_value, stretch_order, doc_lengths):
    hidden = hidden_in[0]
    rows, hd = hidden.shape[0], w_key.shape[1]
    kv, hidden_other = project(hidden, w_key, w_value)
    ctx = lax.axis_index("ctx").astype(jnp.int32).reshape(1)
    query_grad, part = attend(
        stretch_order, doc_lengths[0], ctx, kv.reshape(-1, 2 * hd), queries[0], grad_out[0]
    )
    sums = weight_grads(part.reshape(kv.shape), hidden, hidden_other)

    return query_grad[None], sums[0].astype(F32), sums[1].astype(F32)


def solution(mesh):
    return jax.shard_map(
        on_device,
        mesh=mesh,
        in_specs=(
            P("dp", "ctx", None),
            P("dp", "ctx", None),
            P("dp", "ctx", None),
            P("dp", None),
            P("dp", None),
            P(),
            P("dp", None),
        ),
        out_specs=(P("dp", "ctx", None), P("dp", None), P("dp", None)),
        check_vma=False,
    )
```

```python
import math

import jax
import jax.numpy as jnp
from jax import lax
from jax.experimental import pallas as pl
from jax.experimental.pallas import tpu as pltpu
from jax.sharding import PartitionSpec as P

MESH = pl.DeviceIdType.MESH
SIDE = 4
DEPTH = 8
BF = jnp.bfloat16
F32 = jnp.float32
VMEM_LIMIT = 60 * 2**20
STRETCH = 96
SPAN = 17
FLAT_ROWS = 80


def slot_of(x, y):
    return lax.rem(y, SIDE) * SIDE + lax.rem(x, SIDE)


class Place:
    def __init__(self):
        dp, ctx = lax.axis_index("dp"), lax.axis_index("ctx")
        self.dp, self.ctx = dp, ctx
        self.x, self.y = lax.rem(dp, SIDE), lax.div(dp, SIDE)
        self.z, self.core = lax.div(ctx, 2), lax.rem(ctx, 2)

    def partner(self):
        return (self.dp, self.z * 2 + 1 - self.core)

    def along_z(self, d):
        return (self.dp, lax.rem(self.z + d, DEPTH) * 2 + self.core)

    def along(self, axis, d):
        if axis == 0:
            return (slot_of(self.x + d, self.y), self.ctx)
        return (slot_of(self.x, self.y + d), self.ctx)

    def slot(self, half, du, dv):
        if half == 0:
            return slot_of(self.x + du, self.y + dv)
        return slot_of(self.x + dv, self.y + du)


def greet(devices):
    barrier = pltpu.get_barrier_semaphore()
    for device in devices:
        pl.semaphore_signal(barrier, inc=1, device_id=device, device_id_type=MESH)
    return lambda: pl.semaphore_wait(barrier, len(devices))


class Sender:
    def __init__(self, sems):
        self.sems, self.sent = sems, []

    def __call__(self, src, dst, recv_sem, device):
        copy = pltpu.make_async_remote_copy(
            src_ref=src,
            dst_ref=dst,
            send_sem=self.sems.at[len(self.sent)],
            recv_sem=recv_sem,
            device_id=device,
            device_id_type=MESH,
        )
        copy.start()
        self.sent.append(copy)

    def finish(self):
        for copy in self.sent:
            copy.wait_send()


def arrived(dst, recv_sem, place):
    pltpu.make_async_remote_copy(
        src_ref=dst,
        dst_ref=dst,
        send_sem=recv_sem,
        recv_sem=recv_sem,
        device_id=place.partner(),
        device_id_type=MESH,
    ).wait_recv()


SENDS = 2 * 20 + 1 + 14 + 8 + 8 + 14 + 2 + 32 + 8 + 14 + 7 + 15 + 7 + 8


def kernel(
    hid_ref, q_ref, g_ref, wk_ref, wv_ref, order_ref, where_ref, lens_ref,
    dq_ref, out_ref,
    hbuf, wbuf, acc, pin, pout, kv_ref, qs, gs, kp, kw, scores, dprobs, sums, dqs,
    tb, rout, rbuf, zin, zout, gbuf, gt, pr0, pr1, qr0, qr1, cin, zr, xr,
    s_sem, own_sem, hs_sem, hr_sem, wo_sem, q_sem, go_sem, dq_sem, w_sem, p_sem, z_sem, c_sem,
    d1_sem, d2_sem, d3_sem, p0_sem, p1_sem, q0_sem, q1_sem, n_sem, f_sem, x_sem, g_sem, b_sem,
):
    heads = q_ref.shape[1] // wk_ref.shape[1]
    me = Place()
    all_here = greet(
        [me.partner()]
        + [me.along(a, d) for a in (0, 1) for d in (1, SIDE - 1)]
        + [me.along_z(d) for d in (1, DEPTH - 1)]
    )
    rows, cols, hd = hid_ref.shape[0], wbuf.shape[2], wbuf.shape[3]
    n = SIDE * SIDE

    def part_of(s, core):
        return hid_ref.at[:, pl.ds(pl.multiple_of((s * 2 + core) * cols, cols), cols)]

    def h_copies(s):
        own = pltpu.make_async_copy(part_of(s, me.core), hbuf.at[s, pl.ds(0, rows)], own_sem.at[s])
        other = pltpu.make_async_remote_copy(
            src_ref=part_of(s, 1 - me.core),
            dst_ref=hbuf.at[s, pl.ds(rows, rows)],
            send_sem=hs_sem.at[s],
            recv_sem=hr_sem.at[s],
            device_id=me.partner(),
            device_id_type=MESH,
        )
        return own, other

    mine = pl.ds(pl.multiple_of(me.core * cols, cols), cols)
    w_refs = (wk_ref.at[mine], wv_ref.at[mine])
    w_own = [pltpu.make_async_copy(w_refs[h], wbuf.at[h, me.dp], wo_sem.at[h]) for h in (0, 1)]
    for copy in w_own:
        copy.start()

    def q_copies(i):
        t, h = lax.div(i, heads), lax.rem(i, heads)
        src = (pl.ds(pl.multiple_of(t * STRETCH, STRETCH), STRETCH), pl.ds(pl.multiple_of(h * hd, hd), hd))
        dst = pl.ds(pl.multiple_of(h * STRETCH, STRETCH), STRETCH)
        return (
            pltpu.make_async_copy(q_ref.at[src], qs.at[t, dst], q_sem.at[i]),
            pltpu.make_async_copy(g_ref.at[src], gs.at[t, dst], go_sem.at[i]),
        )

    @pl.loop(0, n)
    def _(i):
        h_copies(slot_of(me.x + lax.rem(i, SIDE), me.y + lax.div(i, SIDE)))[0].start()

    all_here()
    send = Sender(s_sem)

    half_rows = cols // 2
    parts = (pl.ds(0, half_rows), pl.ds(half_rows, half_rows))
    ahead, back = 1, SIDE - 1

    def w_send(h, slot, axis, d, part=None):
        ref = wbuf.at[h, slot]
        sem = w_sem.at[h, slot, 0 if part is None else part]
        if part is not None:
            ref = ref.at[parts[part]]
        send(ref, ref, sem, me.along(axis, d))

    def w_wait(h, slot, part=None):
        ref = wbuf.at[h, slot]
        if part is not None:
            ref = ref.at[parts[part]]
        arrived(ref, w_sem.at[h, slot, 0 if part is None else part], me)

    for d in (ahead, back):
        for h in (0, 1):
            send(w_refs[h], wbuf.at[h, me.dp], w_sem.at[h, me.dp, 0], me.along(h, d))

    for d in (ahead, back):
        for h in (0, 1):
            send(w_refs[h], wbuf.at[h, me.dp], w_sem.at[h, me.dp, 0], me.along(1 - h, d))

    @pl.loop(0, n)
    def _(i):
        h_copies(slot_of(me.x + lax.rem(i, SIDE), me.y + lax.div(i, SIDE)))[1].start()

    acc[...] = jnp.zeros_like(acc)
    for copy in w_own:
        copy.wait()

    def compute(dx, dy):
        s = slot_of(me.x + dx, me.y + dy)
        own, other = h_copies(s)
        own.wait()
        other.wait_recv()
        w = jnp.concatenate([wbuf[0, s], wbuf[1, s]], axis=1)
        acc[...] += jnp.dot(hbuf[s], w, preferred_element_type=F32)

    for d, other, part in ((back, ahead, 0), (ahead, back, 1)):
        for h in (0, 1):
            slot = me.slot(h, d, 0)
            w_wait(h, slot)
            w_send(h, slot, h, other, part)
    for d in (back, ahead):
        for h in (0, 1):
            for e in (ahead, back):
                w_send(h, me.slot(h, d, 0), 1 - h, e)
    compute(0, 0)
    for h in (0, 1):
        slot = me.slot(h, 2, 0)
        w_wait(h, slot, 0)
        w_wait(h, slot, 1)
        for e in (ahead, back):
            w_send(h, slot, 1 - h, e)

    def pass_on(du):
        for d, other, part in ((back, ahead, 0), (ahead, back, 1)):
            for h in (0, 1):
                slot = me.slot(h, du, d)
                w_wait(h, slot)
                w_send(h, slot, 1 - h, other, part)

    pass_on(0)

    @pl.loop(0, 4)
    def _(i):
        a, b = lax.div(i, 2), lax.rem(i, 2)
        compute((1 - a) * (1 + 2 * b), a * (1 + 2 * b))

    pass_on(back)
    pass_on(ahead)

    @pl.loop(0, 4)
    def _(i):
        a, b = lax.div(i, 2), lax.rem(i, 2)
        compute(1 + 2 * a, 1 + 2 * b)

    pass_on(2)

    def far(du):
        for h in (0, 1):
            for part in (0, 1):
                w_wait(h, me.slot(h, du, 2), part)

    far(0)

    @pl.loop(0, 2)
    def _(i):
        compute(2 * i, 2 * (1 - i))

    far(back)
    far(ahead)

    @pl.loop(0, 4)
    def _(i):
        a, b = lax.div(i, 2), lax.rem(i, 2)
        compute((1 - a) * 2 + a * (1 + 2 * b), a * 2 + (1 - a) * (1 + 2 * b))

    far(2)
    compute(2, 2)

    def kv_block(ctx):
        return pl.ds(ctx * 2, 2)

    pout[...] = acc[rows:, :]
    send(pout, pin, p_sem.at[0], me.partner())

    @pl.loop(0, 2 * heads)
    def _(i):
        for copy in q_copies(i):
            copy.start()

    arrived(pin, p_sem.at[0], me)
    kv_ref[kv_block(me.ctx)] = (acc[:rows, :] + pin[...]).astype(BF).reshape(2, STRETCH, 2 * hd)

    def block(d):
        return lax.rem(me.z + d, DEPTH) * 2 + me.core

    half = rows // 2

    def z_part(d, part):
        return kv_ref.at[block(d) * 2 + part]

    def z_send(d, step, part):
        ref, sem = z_part(d, part), z_sem.at[block(d), part]
        send(ref, ref, sem, me.along_z(step))

    def z_wait(d, part):
        arrived(z_part(d, part), z_sem.at[block(d), part], me)

    def share(d):
        ref = kv_ref.at[kv_block(block(d))]
        send(ref, ref, c_sem.at[block(d)], me.partner())

    up, down = 1, DEPTH - 1
    for first in (0, 1):
        z_send(0, up, first)
        z_send(0, down, 1 - first)
    share(0)

    for k in (1, 2, 3):
        for first in (0, 1):
            z_wait(DEPTH - k, first)
            if k < 3 or first == 0:
                z_send(DEPTH - k, up, first)
            z_wait(k, 1 - first)
            if k < 3 or first == 0:
                z_send(k, down, 1 - first)
        share(DEPTH - k)
        share(k)
    z_wait(4, 0)
    z_wait(4, 1)
    share(4)

    @pl.loop(0, DEPTH)
    def _(i):
        other = i * 2 + 1 - me.core
        arrived(kv_ref.at[kv_block(other)], c_sem.at[other], me)


    factor = math.log2(math.e) / math.sqrt(hd)
    scale = 1.0 / math.sqrt(hd)
    width = heads * STRETCH
    nt = (((1,), (1,)), ((), ()))

    def first_of(t):
        return jnp.maximum(order_ref[me.ctx * 2 + t] - (SPAN - 1), 0)

    @pl.loop(0, 2 * heads)
    def _(i):
        for copy in q_copies(i):
            copy.wait()

    @pl.loop(0, where_ref.shape[0])
    def _(i):
        kp[i] = kv_ref[where_ref[i]]

    for t in (0, 1):
        for at in (0, SPAN + 1):
            sums[t, at] = jnp.zeros((STRETCH, 2 * hd), F32)
    inner = slice(1, SPAN + 1)

    @pl.loop(0, 2)
    def _(t):
        place, first = order_ref[me.ctx * 2 + t], first_of(t)

        @pl.loop(0, SPAN)
        def _(i):
            kw[pl.ds(pl.multiple_of(i * STRETCH, STRETCH), STRETCH)] = kp[first + i]

        spot = place * STRETCH + lax.rem(lax.broadcasted_iota(jnp.int32, (1, width), 1), STRETCH)
        low = jnp.zeros_like(spot)
        end = jnp.int32(0)
        for d in range(lens_ref.shape[0]):
            end = end + lens_ref[d]
            low = jnp.where(spot >= end, end, low)
        low, high = low - first * STRETCH, spot - first * STRETCH
        at = lax.broadcasted_iota(jnp.int32, (SPAN * STRETCH, width), 0)
        s = lax.dot_general(kw[:, :hd], qs[t], nt, preferred_element_type=F32)
        s = jnp.where((at >= low) & (at <= high), s, -1e30)
        scores[...] = s
        top = jnp.max(s, axis=0, keepdims=True)
        dprobs[...] = lax.dot_general(kw[:, hd:], gs[t], nt, preferred_element_type=F32)
        e = jnp.exp2((scores[...] - top) * factor)
        scores[...] = e
        inverse = 1.0 / jnp.sum(e, axis=0, keepdims=True)
        delta = jnp.sum(e * dprobs[...], axis=0, keepdims=True) * inverse
        p = scores[...] * inverse
        ds = (p * (dprobs[...] - delta)).astype(BF)
        sums[t, inner, :, :hd] = jnp.dot(ds, qs[t], preferred_element_type=F32).reshape(SPAN, STRETCH, hd)
        sums[t, inner, :, hd:] = jnp.dot(p.astype(BF), gs[t], preferred_element_type=F32).reshape(SPAN, STRETCH, hd)
        dqt = lax.dot_general(kw[:, :hd], ds, (((0,), (0,)), ((), ())), preferred_element_type=F32)
        dq = (jnp.transpose(dqt) * scale).astype(BF)
        row = pl.ds(pl.multiple_of(t * STRETCH, STRETCH), STRETCH)
        for h in range(heads):
            dqs[row, h * hd : (h + 1) * hd] = dq[h * STRETCH : (h + 1) * STRETCH]

    dq_copy = pltpu.make_async_copy(dqs, dq_ref, dq_sem.at[0])
    dq_copy.start()

    def stretch_grads(b):
        total = jnp.zeros((STRETCH, 2 * hd), F32)
        for t in (0, 1):
            i = jnp.minimum(jnp.maximum(order_ref[b] - first_of(t) + 1, 0), SPAN + 1)
            total = total + sums[t, i]
        return jnp.concatenate([total[:, :hd] * scale, total[:, hd:]], axis=1)

    z_steps = (1, DEPTH - 1)

    def z_at(d):
        return lax.rem(me.z + d, DEPTH)

    def target(w, k):
        return 4 - k if w == 0 else DEPTH - 4 + k

    pieces = (pl.ds(0, STRETCH), pl.ds(STRETCH, STRETCH))

    def stretch(d, core, piece):
        return (z_at(d) * 2 + core) * 2 + piece

    for d in (4, 3, 5, 2, 6, 1, 7, 0):
        for piece in (0, 1):
            rout[d, pieces[piece]] = stretch_grads(stretch(d, 1 - me.core, piece)).astype(BF)
        send(rout.at[d], rbuf.at[d], d1_sem.at[d], me.partner())

    known = set()

    def own_sum(d, piece):
        if d not in known:
            known.add(d)
            arrived(rbuf.at[d], d1_sem.at[d], me)
        return stretch_grads(stretch(d, me.core, piece)) + rbuf[d, pieces[piece]].astype(F32)

    def kv_step(w, k, piece, first):
        total = own_sum(target(w, k), piece)
        if not first:
            arrived(zin.at[w, k - 1, pieces[piece]], d2_sem.at[w, k - 1, piece], me)
            total = total + zin[w, k - 1, pieces[piece]].astype(F32)
        ref = zout.at[w, k, pieces[piece]]
        ref[...] = total.astype(BF)
        send(ref, zin.at[w, k, pieces[piece]], d2_sem.at[w, k, piece], me.along_z(z_steps[w]))

    for w in (0, 1):
        kv_step(w, 0, w, True)
    for w in (0, 1):
        kv_step(w, 1, 1 - w, True)
    for k in (1, 2, 3):
        for w in (0, 1):
            kv_step(w, k, w, False)
        if k < 3:
            for w in (0, 1):
                kv_step(w, k + 1, 1 - w, False)
    for piece in (0, 1):
        total = own_sum(0, piece)
        for w in (0, 1):
            arrived(zin.at[w, 3, pieces[piece]], d2_sem.at[w, 3, piece], me)
            total = total + zin[w, 3, pieces[piece]].astype(F32)
        ref = gbuf.at[0, pieces[piece]]
        ref[...] = total.astype(BF)
        send(ref, gbuf.at[1, pieces[piece]], d3_sem.at[piece], me.partner())
    gt[:, :rows] = jnp.transpose(gbuf[0].astype(F32)).astype(BF)

    for piece in (0, 1):
        arrived(gbuf.at[1, pieces[piece]], d3_sem.at[piece], me)
    gt[:, rows:] = jnp.transpose(gbuf[1].astype(F32)).astype(BF)

    groups = DEPTH // 2

    def terms(dx, dy):
        s = slot_of(me.x + dx, me.y + dy)
        t = jnp.dot(gt[...], hbuf[s], preferred_element_type=F32).astype(BF)
        for j in range(DEPTH):
            h, g = divmod(j, groups)
            tb[j, s] = t[h * hd : (h + 1) * hd, g * hd : (g + 1) * hd]

    sides = (1, SIDE - 1)

    def flat(h, slot, dv, w=None):
        cut = 48 if dv % 2 == 0 else 32
        at = pl.ds(0, FLAT_ROWS) if w is None else pl.ds(0, cut) if w == 0 else pl.ds(cut, FLAT_ROWS - cut)
        return tb.at[pl.ds(groups * h, groups), slot, at], at

    def first_sends(h):
        for dv in (2, 1, 3, 0):
            for w in (0, 1):
                ref, at = flat(h, me.slot(h, 2, dv), dv, w)
                send(ref, pr0.at[h, w, dv, :, at], p0_sem.at[h, w, dv], me.along(h, sides[w]))

    @pl.loop(0, SIDE)
    def _(i):
        terms(2, i)

    first_sends(0)

    @pl.loop(0, SIDE - 1)
    def _(i):
        terms(i + lax.div(i, 2), 2)

    first_sends(1)

    @pl.loop(0, (SIDE - 1) * (SIDE - 1))
    def _(i):
        a, b = lax.div(i, 3), lax.rem(i, 3)
        terms(a + lax.div(a, 2), b + lax.div(b, 2))

    def add(ref, *got):
        total = ref[...].astype(F32)
        for g in got:
            total = total + g.astype(F32)
        ref[...] = total.astype(BF)

    deep = pl.ds(FLAT_ROWS, hd - FLAT_ROWS)
    slots = (pl.ds(0, n // 2), pl.ds(n // 2, n // 2))

    def deep_step(k, w, piece, first=False):
        ref = tb.at[z_at(target(w, k)), slots[piece], deep]
        if not first:
            got = cin.at[w, k - 1, slots[piece]]
            arrived(got, n_sem.at[w, k - 1, piece], me)
            add(ref, got[...])
        send(ref, cin.at[w, k, slots[piece]], n_sem.at[w, k, piece], me.along_z(z_steps[w]))

    def second_sends(dv):
        for h in (0, 1):
            for w in (0, 1):
                slot = me.slot(h, sides[w], dv)
                ref, at = flat(h, slot, dv, w)
                got = pr0.at[h, w, dv, :, at]
                arrived(got, p0_sem.at[h, w, dv], me)
                add(ref, got[...])
                send(flat(h, slot, dv)[0], pr1.at[h, w, dv], p1_sem.at[h, w, dv], me.along(h, sides[w]))

    def collect(h, dv):
        for w in (0, 1):
            arrived(pr1.at[h, w, dv], p1_sem.at[h, w, dv], me)
        add(flat(h, me.slot(h, 0, dv), dv)[0], pr1[h, 0, dv], pr1[h, 1, dv])

    def third_sends(h):
        for w in (0, 1):
            ref, at = flat(h, me.slot(h, 0, 2), h, w)
            send(ref, qr0.at[h, w, :, at], q0_sem.at[h, w], me.along(1 - h, sides[w]))

    def fourth_sends(h, w):
        slot = me.slot(h, 0, sides[w])
        ref, at = flat(h, slot, h, w)
        got = qr0.at[h, w, :, at]
        arrived(got, q0_sem.at[h, w], me)
        add(ref, got[...])
        send(flat(h, slot, 0)[0], qr1.at[h, w], q1_sem.at[h, w], me.along(1 - h, sides[w]))

    for w in (0, 1):
        deep_step(0, w, w, True)
    for w in (0, 1):
        deep_step(1, w, 1 - w, True)
    second_sends(2)
    second_sends(1)
    for w in (0, 1):
        deep_step(1, w, w)
    second_sends(3)
    second_sends(0)
    for w in (0, 1):
        deep_step(2, w, 1 - w)
    for h in (0, 1):
        collect(h, 2)
        third_sends(h)
    for w in (0, 1):
        deep_step(2, w, w)
    for w in (0, 1):
        for h in (0, 1):
            collect(h, sides[w])
            fourth_sends(h, w)
    for w in (0, 1):
        deep_step(3, w, 1 - w)
    for h in (0, 1):
        collect(h, 0)
    for w in (0, 1):
        deep_step(3, w, w)
    for h in (0, 1):
        for w in (0, 1):
            arrived(qr1.at[h, w], q1_sem.at[h, w], me)
        add(flat(h, me.dp, 0)[0], qr1[h, 0], qr1[h, 1])
    rows_first = pl.ds(0, FLAT_ROWS)
    for d in (4, 3, 5, 2, 6, 1, 7):
        send(tb.at[z_at(d), me.dp, rows_first], zr.at[d], f_sem.at[d], me.along_z(d))
    for piece in (0, 1):
        ref = tb.at[me.z, slots[piece], deep]
        for w in (0, 1):
            arrived(cin.at[w, 3, slots[piece]], n_sem.at[w, 3, piece], me)
        add(ref, cin[0, 3, slots[piece]], cin[1, 3, slots[piece]])
    for far in range(4, 0, -1):
        for dx in range(SIDE):
            for dy in range(SIDE):
                if min(dx, SIDE - dx) + min(dy, SIDE - dy) == far:
                    slot = slot_of(me.x + dx, me.y + dy)
                    send(tb.at[me.z, slot, deep], xr.at[dy * SIDE + dx], x_sem.at[dy * SIDE + dx], (slot, me.ctx))

    top = tb[me.z, me.dp, rows_first].astype(F32)
    for d in range(1, DEPTH):
        arrived(zr.at[d], f_sem.at[d], me)
        top = top + zr[d].astype(F32)
    low = tb[me.z, me.dp, deep].astype(F32)
    for i in range(1, n):
        arrived(xr.at[i], x_sem.at[i], me)
        low = low + xr[i].astype(F32)
    done = jnp.transpose(jnp.concatenate([top, low], axis=0)).astype(BF)

    def block(d, core):
        j = z_at(d)
        at = core * cols + lax.rem(j, groups) * hd
        return out_ref.at[lax.div(j, groups), pl.ds(pl.multiple_of(at, hd), hd)]

    def share_block(d):
        send(block(d, me.core), block(d, me.core), b_sem.at[d], me.partner())

    block(0, me.core)[...] = done
    for d in (4, 3, 5, 2, 6, 1, 7):
        send(block(0, me.core), block(0, me.core), g_sem.at[d], me.along_z(d))
    share_block(0)
    for d in (1, 7, 2, 6, 3, 5, 4):
        arrived(block(d, me.core), g_sem.at[DEPTH - d], me)
        share_block(d)
    for d in range(DEPTH):
        arrived(block(d, 1 - me.core), b_sem.at[d], me)
    send.finish()
    dq_copy.wait()

    @pl.loop(0, n)
    def _(s):
        h_copies(s)[1].wait_send()


def finish_kernel(dq_ref, sums_ref, dq_out, key_out, value_out):
    dq_out[...] = dq_ref[...]
    key_out[...] = sums_ref[0].astype(F32)
    value_out[...] = sums_ref[1].astype(F32)


def finish(query_grad, sums):
    steps = 4
    (rows, width), (_, depth, hd) = query_grad.shape, sums.shape
    dq_spec = pl.BlockSpec((rows // steps, width), lambda i: (i, 0))
    out_spec = pl.BlockSpec((depth // steps, hd), lambda i: (i, 0))
    return pl.pallas_call(
        finish_kernel,
        grid=(steps,),
        out_shape=(
            jax.ShapeDtypeStruct(query_grad.shape, BF),
            jax.ShapeDtypeStruct((depth, hd), F32),
            jax.ShapeDtypeStruct((depth, hd), F32),
        ),
        in_specs=[dq_spec, pl.BlockSpec((2, depth // steps, hd), lambda i: (0, i, 0))],
        out_specs=(dq_spec, out_spec, out_spec),
        name="finish",
    )(query_grad, sums)


def on_device(hidden_in, queries, grad_out, w_key, w_value, stretch_order, doc_lengths):
    hidden = hidden_in[0]
    rows, hd = hidden.shape[0], w_key.shape[1]
    n = SIDE * SIDE
    cols = hidden.shape[1] // n // 2
    width, span = 2 * hd, SPAN * STRETCH
    heads = queries.shape[2] // hd
    groups = DEPTH // 2
    every = jnp.arange(stretch_order.shape[0], dtype=jnp.int32)
    stored_at = jnp.sum(jnp.where(stretch_order[None, :] == every[:, None], every[None, :], 0), axis=1)
    dma = pltpu.SemaphoreType.DMA
    smem, hbm = pl.BlockSpec(memory_space=pltpu.SMEM), pl.BlockSpec(memory_space=pl.ANY)
    query_grad, sums = pl.pallas_call(
        kernel,
        out_shape=(
            jax.ShapeDtypeStruct((rows, heads * hd), BF),
            jax.ShapeDtypeStruct((2, 2 * cols, hd), BF),
        ),
        in_specs=[hbm] * 5 + [smem] * 3,
        out_specs=(hbm, pl.BlockSpec(memory_space=pltpu.VMEM)),
        scratch_shapes=[
            pltpu.VMEM((n, 2 * rows, cols), BF),
            pltpu.VMEM((2, n, cols, hd), BF),
            pltpu.VMEM((2 * rows, width), F32),
            pltpu.VMEM((rows, width), F32),
            pltpu.VMEM((rows, width), F32),
            pltpu.VMEM((2 * 2 * DEPTH, STRETCH, width), BF),
            pltpu.VMEM((2, heads * STRETCH, hd), BF),
            pltpu.VMEM((2, heads * STRETCH, hd), BF),
            pltpu.VMEM((2 * 2 * DEPTH, STRETCH, width), BF),
            pltpu.VMEM((span, width), BF),
            pltpu.VMEM((span, heads * STRETCH), F32),
            pltpu.VMEM((span, heads * STRETCH), F32),
            pltpu.VMEM((2, SPAN + 2, STRETCH, width), F32),
            pltpu.VMEM((rows, heads * hd), BF),
            pltpu.VMEM((DEPTH, n, hd, hd), BF),
            pltpu.VMEM((DEPTH, rows, width), BF),
            pltpu.VMEM((DEPTH, rows, width), BF),
            pltpu.VMEM((2, 4, rows, width), BF),
            pltpu.VMEM((2, 4, rows, width), BF),
            pltpu.VMEM((2, rows, width), BF),
            pltpu.VMEM((width, 2 * rows), BF),
            pltpu.VMEM((2, 2, SIDE, groups, FLAT_ROWS, hd), BF),
            pltpu.VMEM((2, 2, SIDE, groups, FLAT_ROWS, hd), BF),
            pltpu.VMEM((2, 2, groups, FLAT_ROWS, hd), BF),
            pltpu.VMEM((2, 2, groups, FLAT_ROWS, hd), BF),
            pltpu.VMEM((2, 4, n, hd - FLAT_ROWS, hd), BF),
            pltpu.VMEM((DEPTH, FLAT_ROWS, hd), BF),
            pltpu.VMEM((n, hd - FLAT_ROWS, hd), BF),
            dma((SENDS,)),
            dma((n,)),
            dma((n,)),
            dma((n,)),
            dma((2,)),
            dma((2 * heads,)),
            dma((2 * heads,)),
            dma((1,)),
            dma((2, n, 2)),
            dma((1,)),
            dma((2 * DEPTH, 2)),
            dma((2 * DEPTH,)),
            dma((DEPTH,)),
            dma((2, 4, 2)),
            dma((2,)),
            dma((2, 2, SIDE)),
            dma((2, 2, SIDE)),
            dma((2, 2)),
            dma((2, 2)),
            dma((2, 4, 2)),
            dma((DEPTH,)),
            dma((n,)),
            dma((DEPTH,)),
            dma((DEPTH,)),
        ],
        compiler_params=pltpu.CompilerParams(
            collective_id=0, has_side_effects=True, vmem_limit_bytes=VMEM_LIMIT
        ),
        name="kv_backward",
    )(hidden, queries[0], grad_out[0], w_key, w_value, stretch_order, stored_at, doc_lengths[0])
    query_grad, key_sums, value_sums = finish(query_grad, sums)
    return query_grad[None], key_sums, value_sums


def solution(mesh):
    return jax.shard_map(
        on_device,
        mesh=mesh,
        in_specs=(
            P("dp", "ctx", None),
            P("dp", "ctx", None),
            P("dp", "ctx", None),
            P("dp", None),
            P("dp", None),
            P(),
            P("dp", None),
        ),
        out_specs=(P("dp", "ctx", None), P("dp", None), P("dp", None)),
        check_vma=False,
    )
```

```python
import math

import jax
import jax.numpy as jnp
from jax import lax
from jax.experimental import pallas as pl
from jax.experimental.pallas import tpu as pltpu
from jax.sharding import PartitionSpec as P

MESH = pl.DeviceIdType.MESH
SIDE = 4
DEPTH = 8
BF = jnp.bfloat16
F32 = jnp.float32
VMEM_LIMIT = 60 * 2**20
STRETCH = 96
SPAN = 17
FLAT_ROWS = 80


def slot_of(x, y):
    return lax.rem(y, SIDE) * SIDE + lax.rem(x, SIDE)


class Place:
    def __init__(self):
        dp, ctx = lax.axis_index("dp"), lax.axis_index("ctx")
        self.dp, self.ctx = dp, ctx
        self.x, self.y = lax.rem(dp, SIDE), lax.div(dp, SIDE)
        self.z, self.core = lax.div(ctx, 2), lax.rem(ctx, 2)

    def partner(self):
        return (self.dp, self.z * 2 + 1 - self.core)

    def along_z(self, d):
        return (self.dp, lax.rem(self.z + d, DEPTH) * 2 + self.core)

    def across(self, d):
        return (self.dp, lax.rem(self.z + d, DEPTH) * 2 + 1 - self.core)

    def along(self, axis, d):
        if axis == 0:
            return (slot_of(self.x + d, self.y), self.ctx)
        return (slot_of(self.x, self.y + d), self.ctx)

    def slot(self, half, du, dv):
        if half == 0:
            return slot_of(self.x + du, self.y + dv)
        return slot_of(self.x + dv, self.y + du)


def greet(devices):
    barrier = pltpu.get_barrier_semaphore()
    for device in devices:
        pl.semaphore_signal(barrier, inc=1, device_id=device, device_id_type=MESH)
    return lambda: pl.semaphore_wait(barrier, len(devices))


class Sender:
    def __init__(self, sems):
        self.sems, self.sent = sems, []

    def __call__(self, src, dst, recv_sem, device):
        copy = pltpu.make_async_remote_copy(
            src_ref=src,
            dst_ref=dst,
            send_sem=self.sems.at[len(self.sent)],
            recv_sem=recv_sem,
            device_id=device,
            device_id_type=MESH,
        )
        copy.start()
        self.sent.append(copy)

    def finish(self):
        for copy in self.sent:
            copy.wait_send()


def arrived(dst, recv_sem, place):
    pltpu.make_async_remote_copy(
        src_ref=dst,
        dst_ref=dst,
        send_sem=recv_sem,
        recv_sem=recv_sem,
        device_id=place.partner(),
        device_id_type=MESH,
    ).wait_recv()


SENDS = 2 * 20 + 1 + 14 + 2 + 7 + 8 + 14 + 2 + 32 + 8 + 14 + 7 + 15 + 7 + 8


def kernel(
    hid_ref, q_ref, g_ref, wk_ref, wv_ref, order_ref, lens_ref,
    dq_ref, out_ref,
    hbuf, wbuf, acc, pin, pout, kv_ref, where_ref, qs, gs, kp, kw, scores, dprobs, sums, dqs,
    tb, rout, rbuf, zin, zout, gbuf, gt, pr0, pr1, qr0, qr1, cin, zr, xr,
    s_sem, own_sem, hs_sem, hr_sem, wo_sem, q_sem, go_sem, dq_sem, w_sem, p_sem, z_sem, c_sem, e_sem,
    d1_sem, d2_sem, d3_sem, p0_sem, p1_sem, q0_sem, q1_sem, n_sem, f_sem, x_sem, g_sem, b_sem,
):
    heads = q_ref.shape[1] // wk_ref.shape[1]
    me = Place()
    all_here = greet(
        [me.partner()]
        + [me.along(a, d) for a in (0, 1) for d in (1, SIDE - 1)]
        + [me.along_z(d) for d in (1, DEPTH - 1)]
    )
    rows, cols, hd = hid_ref.shape[0], wbuf.shape[2], wbuf.shape[3]
    n = SIDE * SIDE

    def part_of(s, core):
        return hid_ref.at[:, pl.ds(pl.multiple_of((s * 2 + core) * cols, cols), cols)]

    def h_copies(s):
        own = pltpu.make_async_copy(part_of(s, me.core), hbuf.at[s, pl.ds(0, rows)], own_sem.at[s])
        other = pltpu.make_async_remote_copy(
            src_ref=part_of(s, 1 - me.core),
            dst_ref=hbuf.at[s, pl.ds(rows, rows)],
            send_sem=hs_sem.at[s],
            recv_sem=hr_sem.at[s],
            device_id=me.partner(),
            device_id_type=MESH,
        )
        return own, other

    mine = pl.ds(pl.multiple_of(me.core * cols, cols), cols)
    w_refs = (wk_ref.at[mine], wv_ref.at[mine])
    w_own = [pltpu.make_async_copy(w_refs[h], wbuf.at[h, me.dp], wo_sem.at[h]) for h in (0, 1)]
    for copy in w_own:
        copy.start()

    def q_copies(i):
        t, h = lax.div(i, heads), lax.rem(i, heads)
        src = (pl.ds(pl.multiple_of(t * STRETCH, STRETCH), STRETCH), pl.ds(pl.multiple_of(h * hd, hd), hd))
        dst = pl.ds(pl.multiple_of(h * STRETCH, STRETCH), STRETCH)
        return (
            pltpu.make_async_copy(q_ref.at[src], qs.at[t, dst], q_sem.at[i]),
            pltpu.make_async_copy(g_ref.at[src], gs.at[t, dst], go_sem.at[i]),
        )

    @pl.loop(0, n)
    def _(i):
        h_copies(slot_of(me.x + lax.rem(i, SIDE), me.y + lax.div(i, SIDE)))[0].start()

    for copy in w_own:
        copy.wait()
    all_here()
    send = Sender(s_sem)

    half_rows = cols // 2
    parts = (pl.ds(0, half_rows), pl.ds(half_rows, half_rows))
    ahead, back = 1, SIDE - 1

    def w_send(h, slot, axis, d, part=None):
        ref = wbuf.at[h, slot]
        sem = w_sem.at[h, slot, 0 if part is None else part]
        if part is not None:
            ref = ref.at[parts[part]]
        send(ref, ref, sem, me.along(axis, d))

    def w_wait(h, slot, part=None):
        ref = wbuf.at[h, slot]
        if part is not None:
            ref = ref.at[parts[part]]
        arrived(ref, w_sem.at[h, slot, 0 if part is None else part], me)

    for d in (ahead, back):
        for h in (0, 1):
            w_send(h, me.dp, h, d)

    for d in (ahead, back):
        for h in (0, 1):
            w_send(h, me.dp, 1 - h, d)

    @pl.loop(0, n)
    def _(i):
        h_copies(slot_of(me.x + lax.rem(i, SIDE), me.y + lax.div(i, SIDE)))[1].start()

    acc[...] = jnp.zeros_like(acc)

    def compute(dx, dy):
        s = slot_of(me.x + dx, me.y + dy)
        own, other = h_copies(s)
        own.wait()
        other.wait_recv()
        w = jnp.concatenate([wbuf[0, s], wbuf[1, s]], axis=1)
        acc[...] += jnp.dot(hbuf[s], w, preferred_element_type=F32)

    for d, other, part in ((back, ahead, 0), (ahead, back, 1)):
        for h in (0, 1):
            slot = me.slot(h, d, 0)
            w_wait(h, slot)
            w_send(h, slot, h, other, part)
    for d in (back, ahead):
        for h in (0, 1):
            for e in (ahead, back):
                w_send(h, me.slot(h, d, 0), 1 - h, e)
    compute(0, 0)
    for h in (0, 1):
        slot = me.slot(h, 2, 0)
        w_wait(h, slot, 0)
        w_wait(h, slot, 1)
        for e in (ahead, back):
            w_send(h, slot, 1 - h, e)

    def pass_on(du):
        for d, other, part in ((back, ahead, 0), (ahead, back, 1)):
            for h in (0, 1):
                slot = me.slot(h, du, d)
                w_wait(h, slot)
                w_send(h, slot, 1 - h, other, part)

    pass_on(0)

    @pl.loop(0, 4)
    def _(i):
        a, b = lax.div(i, 2), lax.rem(i, 2)
        compute((1 - a) * (1 + 2 * b), a * (1 + 2 * b))

    pass_on(back)
    pass_on(ahead)

    @pl.loop(0, 4)
    def _(i):
        a, b = lax.div(i, 2), lax.rem(i, 2)
        compute(1 + 2 * a, 1 + 2 * b)

    pass_on(2)

    def far(du):
        for h in (0, 1):
            for part in (0, 1):
                w_wait(h, me.slot(h, du, 2), part)

    far(0)

    @pl.loop(0, 2)
    def _(i):
        compute(2 * i, 2 * (1 - i))

    far(back)
    far(ahead)

    @pl.loop(0, 4)
    def _(i):
        a, b = lax.div(i, 2), lax.rem(i, 2)
        compute((1 - a) * 2 + a * (1 + 2 * b), a * 2 + (1 - a) * (1 + 2 * b))

    far(2)
    compute(2, 2)

    def kv_block(ctx):
        return pl.ds(ctx * 2, 2)

    pout[...] = acc[rows:, :]
    send(pout, pin, p_sem.at[0], me.partner())

    @pl.loop(0, 2 * heads)
    def _(i):
        for copy in q_copies(i):
            copy.start()

    arrived(pin, p_sem.at[0], me)
    kv_ref[kv_block(me.ctx)] = (acc[:rows, :] + pin[...]).astype(BF).reshape(2, STRETCH, 2 * hd)

    def block(d):
        return lax.rem(me.z + d, DEPTH) * 2 + me.core

    half = rows // 2

    def z_part(d, part):
        return kv_ref.at[block(d) * 2 + part]

    def z_send(d, step, part):
        ref, sem = z_part(d, part), z_sem.at[block(d), part]
        send(ref, ref, sem, me.along_z(step))

    def z_wait(d, part):
        arrived(z_part(d, part), z_sem.at[block(d), part], me)

    def share(d):
        ref = kv_ref.at[kv_block(block(d))]
        send(ref, ref, c_sem.at[block(d)], me.partner())

    up, down = 1, DEPTH - 1
    for first in (0, 1):
        z_send(0, up, first)
        z_send(0, down, 1 - first)
    share(0)

    n_stretch = order_ref.shape[0]

    @pl.loop(0, n_stretch)
    def _(i):
        at = jnp.int32(0)
        for b in range(n_stretch):
            at = jnp.where(order_ref[b] == i, b, at)
        where_ref[i] = at

    for k in (1, 2, 3):
        for first in (0, 1):
            z_wait(DEPTH - k, first)
            if k < 3 or first == 0:
                z_send(DEPTH - k, up, first)
            z_wait(k, 1 - first)
            if k < 3 or first == 0:
                z_send(k, down, 1 - first)
        if k == 3:
            for d, step, part in ((DEPTH - 3, up, 0), (3, down, 1)):
                ref = z_part(d, part)
                send(ref, ref, e_sem.at[part], me.across(step))
        share(DEPTH - k)
        share(k)
    z_wait(4, 0)
    z_wait(4, 1)
    for d in range(DEPTH):
        other = lax.rem(me.z + d, DEPTH) * 2 + 1 - me.core
        if d == 4:
            for part in (0, 1):
                arrived(kv_ref.at[other * 2 + part], e_sem.at[part], me)
        else:
            arrived(kv_ref.at[kv_block(other)], c_sem.at[other], me)

    factor = math.log2(math.e) / math.sqrt(hd)
    scale = 1.0 / math.sqrt(hd)
    width = heads * STRETCH
    nt = (((1,), (1,)), ((), ()))

    def first_of(t):
        return jnp.maximum(order_ref[me.ctx * 2 + t] - (SPAN - 1), 0)

    @pl.loop(0, 2 * heads)
    def _(i):
        for copy in q_copies(i):
            copy.wait()

    @pl.loop(0, where_ref.shape[0])
    def _(i):
        kp[i] = kv_ref[where_ref[i]]

    for t in (0, 1):
        for at in (0, SPAN + 1):
            sums[t, at] = jnp.zeros((STRETCH, 2 * hd), F32)
    inner = slice(1, SPAN + 1)

    @pl.loop(0, 2)
    def _(t):
        place, first = order_ref[me.ctx * 2 + t], first_of(t)

        @pl.loop(0, SPAN)
        def _(i):
            kw[pl.ds(pl.multiple_of(i * STRETCH, STRETCH), STRETCH)] = kp[first + i]

        spot = place * STRETCH + lax.rem(lax.broadcasted_iota(jnp.int32, (1, width), 1), STRETCH)
        low = jnp.zeros_like(spot)
        end = jnp.int32(0)
        for d in range(lens_ref.shape[0]):
            end = end + lens_ref[d]
            low = jnp.where(spot >= end, end, low)
        low, high = low - first * STRETCH, spot - first * STRETCH
        at = lax.broadcasted_iota(jnp.int32, (SPAN * STRETCH, width), 0)
        s = lax.dot_general(kw[:, :hd], qs[t], nt, preferred_element_type=F32)
        s = jnp.where((at >= low) & (at <= high), s, -1e30)
        scores[...] = s
        top = jnp.max(s, axis=0, keepdims=True)
        dprobs[...] = lax.dot_general(kw[:, hd:], gs[t], nt, preferred_element_type=F32)
        e = jnp.exp2((scores[...] - top) * factor)
        scores[...] = e
        inverse = 1.0 / jnp.sum(e, axis=0, keepdims=True)
        delta = jnp.sum(e * dprobs[...], axis=0, keepdims=True) * inverse
        p = scores[...] * inverse
        ds = (p * (dprobs[...] - delta)).astype(BF)
        sums[t, inner, :, :hd] = jnp.dot(ds, qs[t], preferred_element_type=F32).reshape(SPAN, STRETCH, hd)
        sums[t, inner, :, hd:] = jnp.dot(p.astype(BF), gs[t], preferred_element_type=F32).reshape(SPAN, STRETCH, hd)
        dqt = lax.dot_general(kw[:, :hd], ds, (((0,), (0,)), ((), ())), preferred_element_type=F32)
        dq = (jnp.transpose(dqt) * scale).astype(BF)
        row = pl.ds(pl.multiple_of(t * STRETCH, STRETCH), STRETCH)
        for h in range(heads):
            dqs[row, h * hd : (h + 1) * hd] = dq[h * STRETCH : (h + 1) * STRETCH]

    dq_copy = pltpu.make_async_copy(dqs, dq_ref, dq_sem.at[0])
    dq_copy.start()

    def stretch_grads(b):
        total = jnp.zeros((STRETCH, 2 * hd), F32)
        for t in (0, 1):
            i = jnp.minimum(jnp.maximum(order_ref[b] - first_of(t) + 1, 0), SPAN + 1)
            total = total + sums[t, i]
        return jnp.concatenate([total[:, :hd] * scale, total[:, hd:]], axis=1)

    z_steps = (1, DEPTH - 1)

    def z_at(d):
        return lax.rem(me.z + d, DEPTH)

    def target(w, k):
        return 4 - k if w == 0 else DEPTH - 4 + k

    pieces = (pl.ds(0, STRETCH), pl.ds(STRETCH, STRETCH))

    def stretch(d, core, piece):
        return (z_at(d) * 2 + core) * 2 + piece

    for d in (4, 3, 5, 2, 6, 1, 7, 0):
        for piece in (0, 1):
            rout[d, pieces[piece]] = stretch_grads(stretch(d, 1 - me.core, piece)).astype(BF)
        send(rout.at[d], rbuf.at[d], d1_sem.at[d], me.partner())

    known = set()

    def own_sum(d, piece):
        if d not in known:
            known.add(d)
            arrived(rbuf.at[d], d1_sem.at[d], me)
        return stretch_grads(stretch(d, me.core, piece)) + rbuf[d, pieces[piece]].astype(F32)

    def kv_step(w, k, piece, first):
        total = own_sum(target(w, k), piece)
        if not first:
            arrived(zin.at[w, k - 1, pieces[piece]], d2_sem.at[w, k - 1, piece], me)
            total = total + zin[w, k - 1, pieces[piece]].astype(F32)
        ref = zout.at[w, k, pieces[piece]]
        ref[...] = total.astype(BF)
        send(ref, zin.at[w, k, pieces[piece]], d2_sem.at[w, k, piece], me.along_z(z_steps[w]))

    for w in (0, 1):
        kv_step(w, 0, w, True)
    for w in (0, 1):
        kv_step(w, 1, 1 - w, True)
    for k in (1, 2, 3):
        for w in (0, 1):
            kv_step(w, k, w, False)
        if k < 3:
            for w in (0, 1):
                kv_step(w, k + 1, 1 - w, False)
    for piece in (0, 1):
        total = own_sum(0, piece)
        for w in (0, 1):
            arrived(zin.at[w, 3, pieces[piece]], d2_sem.at[w, 3, piece], me)
            total = total + zin[w, 3, pieces[piece]].astype(F32)
        ref = gbuf.at[0, pieces[piece]]
        ref[...] = total.astype(BF)
        send(ref, gbuf.at[1, pieces[piece]], d3_sem.at[piece], me.partner())
    gt[:, :rows] = jnp.transpose(gbuf[0].astype(F32)).astype(BF)

    for piece in (0, 1):
        arrived(gbuf.at[1, pieces[piece]], d3_sem.at[piece], me)
    gt[:, rows:] = jnp.transpose(gbuf[1].astype(F32)).astype(BF)

    groups = DEPTH // 2

    def terms(dx, dy):
        s = slot_of(me.x + dx, me.y + dy)
        t = jnp.dot(gt[...], hbuf[s], preferred_element_type=F32).astype(BF)
        for j in range(DEPTH):
            h, g = divmod(j, groups)
            tb[j, s] = t[h * hd : (h + 1) * hd, g * hd : (g + 1) * hd]

    sides = (1, SIDE - 1)

    def flat(h, slot, dv, w=None):
        cut = 48 if dv % 2 == 0 else 32
        at = pl.ds(0, FLAT_ROWS) if w is None else pl.ds(0, cut) if w == 0 else pl.ds(cut, FLAT_ROWS - cut)
        return tb.at[pl.ds(groups * h, groups), slot, at], at

    def first_sends(h):
        for dv in (2, 1, 3, 0):
            for w in (0, 1):
                ref, at = flat(h, me.slot(h, 2, dv), dv, w)
                send(ref, pr0.at[h, w, dv, :, at], p0_sem.at[h, w, dv], me.along(h, sides[w]))

    @pl.loop(0, SIDE)
    def _(i):
        terms(2, i)

    first_sends(0)

    @pl.loop(0, SIDE - 1)
    def _(i):
        terms(i + lax.div(i, 2), 2)

    first_sends(1)

    @pl.loop(0, (SIDE - 1) * (SIDE - 1))
    def _(i):
        a, b = lax.div(i, 3), lax.rem(i, 3)
        terms(a + lax.div(a, 2), b + lax.div(b, 2))

    def add(ref, *got):
        total = ref[...].astype(F32)
        for g in got:
            total = total + g.astype(F32)
        ref[...] = total.astype(BF)

    deep = pl.ds(FLAT_ROWS, hd - FLAT_ROWS)
    slots = (pl.ds(0, n // 2), pl.ds(n // 2, n // 2))

    def deep_step(k, w, piece, first=False):
        ref = tb.at[z_at(target(w, k)), slots[piece], deep]
        if not first:
            got = cin.at[w, k - 1, slots[piece]]
            arrived(got, n_sem.at[w, k - 1, piece], me)
            add(ref, got[...])
        send(ref, cin.at[w, k, slots[piece]], n_sem.at[w, k, piece], me.along_z(z_steps[w]))

    def second_sends(dv):
        for h in (0, 1):
            for w in (0, 1):
                slot = me.slot(h, sides[w], dv)
                ref, at = flat(h, slot, dv, w)
                got = pr0.at[h, w, dv, :, at]
                arrived(got, p0_sem.at[h, w, dv], me)
                add(ref, got[...])
                send(flat(h, slot, dv)[0], pr1.at[h, w, dv], p1_sem.at[h, w, dv], me.along(h, sides[w]))

    def collect(h, dv):
        for w in (0, 1):
            arrived(pr1.at[h, w, dv], p1_sem.at[h, w, dv], me)
        add(flat(h, me.slot(h, 0, dv), dv)[0], pr1[h, 0, dv], pr1[h, 1, dv])

    def third_sends(h):
        for w in (0, 1):
            ref, at = flat(h, me.slot(h, 0, 2), h, w)
            send(ref, qr0.at[h, w, :, at], q0_sem.at[h, w], me.along(1 - h, sides[w]))

    def fourth_sends(h, w):
        slot = me.slot(h, 0, sides[w])
        ref, at = flat(h, slot, h, w)
        got = qr0.at[h, w, :, at]
        arrived(got, q0_sem.at[h, w], me)
        add(ref, got[...])
        send(flat(h, slot, 0)[0], qr1.at[h, w], q1_sem.at[h, w], me.along(1 - h, sides[w]))

    for w in (0, 1):
        deep_step(0, w, w, True)
    for w in (0, 1):
        deep_step(1, w, 1 - w, True)
    second_sends(2)
    second_sends(1)
    for w in (0, 1):
        deep_step(1, w, w)
    second_sends(3)
    second_sends(0)
    for w in (0, 1):
        deep_step(2, w, 1 - w)
    for h in (0, 1):
        collect(h, 2)
        third_sends(h)
    for w in (0, 1):
        deep_step(2, w, w)
    for w in (0, 1):
        for h in (0, 1):
            collect(h, sides[w])
            fourth_sends(h, w)
    for w in (0, 1):
        deep_step(3, w, 1 - w)
    for h in (0, 1):
        collect(h, 0)
    for w in (0, 1):
        deep_step(3, w, w)
    for h in (0, 1):
        for w in (0, 1):
            arrived(qr1.at[h, w], q1_sem.at[h, w], me)
        add(flat(h, me.dp, 0)[0], qr1[h, 0], qr1[h, 1])
    rows_first = pl.ds(0, FLAT_ROWS)
    for d in (4, 3, 5, 2, 6, 1, 7):
        send(tb.at[z_at(d), me.dp, rows_first], zr.at[d], f_sem.at[d], me.along_z(d))
    for piece in (0, 1):
        ref = tb.at[me.z, slots[piece], deep]
        for w in (0, 1):
            arrived(cin.at[w, 3, slots[piece]], n_sem.at[w, 3, piece], me)
        add(ref, cin[0, 3, slots[piece]], cin[1, 3, slots[piece]])
    for far in range(4, 0, -1):
        for dx in range(SIDE):
            for dy in range(SIDE):
                if min(dx, SIDE - dx) + min(dy, SIDE - dy) == far:
                    slot = slot_of(me.x + dx, me.y + dy)
                    send(tb.at[me.z, slot, deep], xr.at[dy * SIDE + dx], x_sem.at[dy * SIDE + dx], (slot, me.ctx))

    top = tb[me.z, me.dp, rows_first].astype(F32)
    for d in range(1, DEPTH):
        arrived(zr.at[d], f_sem.at[d], me)
        top = top + zr[d].astype(F32)
    low = tb[me.z, me.dp, deep].astype(F32)
    for i in range(1, n):
        arrived(xr.at[i], x_sem.at[i], me)
        low = low + xr[i].astype(F32)
    done = jnp.transpose(jnp.concatenate([top, low], axis=0)).astype(BF)

    def block(d, core):
        j = z_at(d)
        at = core * cols + lax.rem(j, groups) * hd
        return out_ref.at[lax.div(j, groups), pl.ds(pl.multiple_of(at, hd), hd)]

    def share_block(d):
        send(block(d, me.core), block(d, me.core), b_sem.at[d], me.partner())

    block(0, me.core)[...] = done
    for d in (4, 3, 5, 2, 6, 1, 7):
        send(block(0, me.core), block(0, me.core), g_sem.at[d], me.along_z(d))
    share_block(0)
    for d in (1, 7, 2, 6, 3, 5, 4):
        arrived(block(d, me.core), g_sem.at[DEPTH - d], me)
        share_block(d)
    for d in range(DEPTH):
        arrived(block(d, 1 - me.core), b_sem.at[d], me)
    send.finish()
    dq_copy.wait()

    @pl.loop(0, n)
    def _(s):
        h_copies(s)[1].wait_send()


def finish_kernel(dq_ref, sums_ref, dq_out, key_out, value_out):
    dq_out[...] = dq_ref[...]
    key_out[...] = sums_ref[0].astype(F32)
    value_out[...] = sums_ref[1].astype(F32)


def finish(query_grad, sums):
    steps = 2
    (rows, width), (_, depth, hd) = query_grad.shape, sums.shape
    dq_spec = pl.BlockSpec((rows // steps, width), lambda i: (i, 0))
    out_spec = pl.BlockSpec((depth // steps, hd), lambda i: (i, 0))
    return pl.pallas_call(
        finish_kernel,
        grid=(steps,),
        out_shape=(
            jax.ShapeDtypeStruct(query_grad.shape, BF),
            jax.ShapeDtypeStruct((depth, hd), F32),
            jax.ShapeDtypeStruct((depth, hd), F32),
        ),
        in_specs=[dq_spec, pl.BlockSpec((2, depth // steps, hd), lambda i: (0, i, 0))],
        out_specs=(dq_spec, out_spec, out_spec),
        name="finish",
    )(query_grad, sums)


def on_device(hidden_in, queries, grad_out, w_key, w_value, stretch_order, doc_lengths):
    hidden = hidden_in[0]
    rows, hd = hidden.shape[0], w_key.shape[1]
    n = SIDE * SIDE
    cols = hidden.shape[1] // n // 2
    width, span = 2 * hd, SPAN * STRETCH
    heads = queries.shape[2] // hd
    groups = DEPTH // 2
    dma = pltpu.SemaphoreType.DMA
    smem, hbm = pl.BlockSpec(memory_space=pltpu.SMEM), pl.BlockSpec(memory_space=pl.ANY)
    query_grad, sums = pl.pallas_call(
        kernel,
        out_shape=(
            jax.ShapeDtypeStruct((rows, heads * hd), BF),
            jax.ShapeDtypeStruct((2, 2 * cols, hd), BF),
        ),
        in_specs=[hbm] * 5 + [smem] * 2,
        out_specs=(hbm, pl.BlockSpec(memory_space=pltpu.VMEM)),
        scratch_shapes=[
            pltpu.VMEM((n, 2 * rows, cols), BF),
            pltpu.VMEM((2, n, cols, hd), BF),
            pltpu.VMEM((2 * rows, width), F32),
            pltpu.VMEM((rows, width), F32),
            pltpu.VMEM((rows, width), F32),
            pltpu.VMEM((2 * 2 * DEPTH, STRETCH, width), BF),
            pltpu.SMEM(stretch_order.shape, jnp.int32),
            pltpu.VMEM((2, heads * STRETCH, hd), BF),
            pltpu.VMEM((2, heads * STRETCH, hd), BF),
            pltpu.VMEM((2 * 2 * DEPTH, STRETCH, width), BF),
            pltpu.VMEM((span, width), BF),
            pltpu.VMEM((span, heads * STRETCH), F32),
            pltpu.VMEM((span, heads * STRETCH), F32),
            pltpu.VMEM((2, SPAN + 2, STRETCH, width), F32),
            pltpu.VMEM((rows, heads * hd), BF),
            pltpu.VMEM((DEPTH, n, hd, hd), BF),
            pltpu.VMEM((DEPTH, rows, width), BF),
            pltpu.VMEM((DEPTH, rows, width), BF),
            pltpu.VMEM((2, 4, rows, width), BF),
            pltpu.VMEM((2, 4, rows, width), BF),
            pltpu.VMEM((2, rows, width), BF),
            pltpu.VMEM((width, 2 * rows), BF),
            pltpu.VMEM((2, 2, SIDE, groups, FLAT_ROWS, hd), BF),
            pltpu.VMEM((2, 2, SIDE, groups, FLAT_ROWS, hd), BF),
            pltpu.VMEM((2, 2, groups, FLAT_ROWS, hd), BF),
            pltpu.VMEM((2, 2, groups, FLAT_ROWS, hd), BF),
            pltpu.VMEM((2, 4, n, hd - FLAT_ROWS, hd), BF),
            pltpu.VMEM((DEPTH, FLAT_ROWS, hd), BF),
            pltpu.VMEM((n, hd - FLAT_ROWS, hd), BF),
            dma((SENDS,)),
            dma((n,)),
            dma((n,)),
            dma((n,)),
            dma((2,)),
            dma((2 * heads,)),
            dma((2 * heads,)),
            dma((1,)),
            dma((2, n, 2)),
            dma((1,)),
            dma((2 * DEPTH, 2)),
            dma((2 * DEPTH,)),
            dma((2,)),
            dma((DEPTH,)),
            dma((2, 4, 2)),
            dma((2,)),
            dma((2, 2, SIDE)),
            dma((2, 2, SIDE)),
            dma((2, 2)),
            dma((2, 2)),
            dma((2, 4, 2)),
            dma((DEPTH,)),
            dma((n,)),
            dma((DEPTH,)),
            dma((DEPTH,)),
        ],
        compiler_params=pltpu.CompilerParams(
            collective_id=0, has_side_effects=True, vmem_limit_bytes=VMEM_LIMIT
        ),
        name="kv_backward",
    )(hidden, queries[0], grad_out[0], w_key, w_value, stretch_order, doc_lengths[0])
    query_grad, key_sums, value_sums = finish(query_grad, sums)
    return query_grad[None], key_sums, value_sums


def solution(mesh):
    return jax.shard_map(
        on_device,
        mesh=mesh,
        in_specs=(
            P("dp", "ctx", None),
            P("dp", "ctx", None),
            P("dp", "ctx", None),
            P("dp", None),
            P("dp", None),
            P(),
            P("dp", None),
        ),
        out_specs=(P("dp", "ctx", None), P("dp", None), P("dp", None)),
        check_vma=False,
    )
```

```python
import math

import jax
import jax.numpy as jnp
from jax import lax
from jax.experimental import pallas as pl
from jax.experimental.pallas import tpu as pltpu
from jax.sharding import PartitionSpec as P

MESH = pl.DeviceIdType.MESH
SIDE = 4
DEPTH = 8
BF = jnp.bfloat16
F32 = jnp.float32
VMEM_LIMIT = 60 * 2**20
STRETCH = 96
SPAN = 17
FLAT_ROWS = 80


def slot_of(x, y):
    return lax.rem(y, SIDE) * SIDE + lax.rem(x, SIDE)


class Place:
    def __init__(self):
        dp, ctx = lax.axis_index("dp"), lax.axis_index("ctx")
        self.dp, self.ctx = dp, ctx
        self.x, self.y = lax.rem(dp, SIDE), lax.div(dp, SIDE)
        self.z, self.core = lax.div(ctx, 2), lax.rem(ctx, 2)

    def partner(self):
        return (self.dp, self.z * 2 + 1 - self.core)

    def along_z(self, d):
        return (self.dp, lax.rem(self.z + d, DEPTH) * 2 + self.core)

    def across(self, d):
        return (self.dp, lax.rem(self.z + d, DEPTH) * 2 + 1 - self.core)

    def along(self, axis, d):
        if axis == 0:
            return (slot_of(self.x + d, self.y), self.ctx)
        return (slot_of(self.x, self.y + d), self.ctx)

    def slot(self, half, du, dv):
        if half == 0:
            return slot_of(self.x + du, self.y + dv)
        return slot_of(self.x + dv, self.y + du)


def greet(devices):
    barrier = pltpu.get_barrier_semaphore()
    for device in devices:
        pl.semaphore_signal(barrier, inc=1, device_id=device, device_id_type=MESH)
    return lambda: pl.semaphore_wait(barrier, len(devices))


class Sender:
    def __init__(self, sems):
        self.sems, self.sent = sems, []

    def __call__(self, src, dst, recv_sem, device):
        copy = pltpu.make_async_remote_copy(
            src_ref=src,
            dst_ref=dst,
            send_sem=self.sems.at[len(self.sent)],
            recv_sem=recv_sem,
            device_id=device,
            device_id_type=MESH,
        )
        copy.start()
        self.sent.append(copy)

    def finish(self):
        for copy in self.sent:
            copy.wait_send()


def arrived(dst, recv_sem, place):
    pltpu.make_async_remote_copy(
        src_ref=dst,
        dst_ref=dst,
        send_sem=recv_sem,
        recv_sem=recv_sem,
        device_id=place.partner(),
        device_id_type=MESH,
    ).wait_recv()


SENDS = 2 * 20 + 1 + 14 + 2 + 7 + 8 + 14 + 2 + 32 + 8 + 14 + 7 + 15 + 7 + 8


def kernel(
    hid_ref, q_ref, g_ref, wk_ref, wv_ref, order_ref, lens_ref,
    dq_ref, out_ref,
    hbuf, wbuf, acc, pin, pout, kv_ref, where_ref, qs, gs, kw, scores, dprobs, sums, dqs,
    tb, rout, rbuf, zin, zout, gbuf, gt, pr0, pr1, qr0, qr1, cin, zr, xr,
    s_sem, own_sem, hs_sem, hr_sem, wo_sem, q_sem, go_sem, dq_sem, w_sem, p_sem, z_sem, c_sem, e_sem,
    d1_sem, d2_sem, d3_sem, p0_sem, p1_sem, q0_sem, q1_sem, n_sem, f_sem, x_sem, g_sem, b_sem,
):
    heads = q_ref.shape[1] // wk_ref.shape[1]
    me = Place()
    all_here = greet(
        [me.partner()]
        + [me.along(a, d) for a in (0, 1) for d in (1, SIDE - 1)]
        + [me.along_z(d) for d in (1, DEPTH - 1)]
    )
    rows, cols, hd = hid_ref.shape[0], wbuf.shape[2], wbuf.shape[3]
    n = SIDE * SIDE

    def part_of(s, core):
        return hid_ref.at[:, pl.ds(pl.multiple_of((s * 2 + core) * cols, cols), cols)]

    def h_copies(s):
        own = pltpu.make_async_copy(part_of(s, me.core), hbuf.at[s, pl.ds(0, rows)], own_sem.at[s])
        other = pltpu.make_async_remote_copy(
            src_ref=part_of(s, 1 - me.core),
            dst_ref=hbuf.at[s, pl.ds(rows, rows)],
            send_sem=hs_sem.at[s],
            recv_sem=hr_sem.at[s],
            device_id=me.partner(),
            device_id_type=MESH,
        )
        return own, other

    mine = pl.ds(pl.multiple_of(me.core * cols, cols), cols)
    w_refs = (wk_ref.at[mine], wv_ref.at[mine])
    w_own = [pltpu.make_async_copy(w_refs[h], wbuf.at[h, me.dp], wo_sem.at[h]) for h in (0, 1)]
    for copy in w_own:
        copy.start()

    def q_copies(i):
        t, h = lax.div(i, heads), lax.rem(i, heads)
        src = (pl.ds(pl.multiple_of(t * STRETCH, STRETCH), STRETCH), pl.ds(pl.multiple_of(h * hd, hd), hd))
        dst = pl.ds(pl.multiple_of(h * STRETCH, STRETCH), STRETCH)
        return (
            pltpu.make_async_copy(q_ref.at[src], qs.at[t, dst], q_sem.at[i]),
            pltpu.make_async_copy(g_ref.at[src], gs.at[t, dst], go_sem.at[i]),
        )

    @pl.loop(0, n)
    def _(i):
        h_copies(slot_of(me.x + lax.rem(i, SIDE), me.y + lax.div(i, SIDE)))[0].start()

    for copy in w_own:
        copy.wait()
    all_here()
    send = Sender(s_sem)

    half_rows = cols // 2
    parts = (pl.ds(0, half_rows), pl.ds(half_rows, half_rows))
    ahead, back = 1, SIDE - 1

    def w_send(h, slot, axis, d, part=None):
        ref = wbuf.at[h, slot]
        sem = w_sem.at[h, slot, 0 if part is None else part]
        if part is not None:
            ref = ref.at[parts[part]]
        send(ref, ref, sem, me.along(axis, d))

    def w_wait(h, slot, part=None):
        ref = wbuf.at[h, slot]
        if part is not None:
            ref = ref.at[parts[part]]
        arrived(ref, w_sem.at[h, slot, 0 if part is None else part], me)

    for d in (ahead, back):
        for h in (0, 1):
            w_send(h, me.dp, h, d)

    for d in (ahead, back):
        for h in (0, 1):
            w_send(h, me.dp, 1 - h, d)

    @pl.loop(0, n)
    def _(i):
        h_copies(slot_of(me.x + lax.rem(i, SIDE), me.y + lax.div(i, SIDE)))[1].start()

    acc[...] = jnp.zeros_like(acc)

    def compute(dx, dy):
        s = slot_of(me.x + dx, me.y + dy)
        own, other = h_copies(s)
        own.wait()
        other.wait_recv()
        w = jnp.concatenate([wbuf[0, s], wbuf[1, s]], axis=1)
        acc[...] += jnp.dot(hbuf[s], w, preferred_element_type=F32)

    for d, other, part in ((back, ahead, 0), (ahead, back, 1)):
        for h in (0, 1):
            slot = me.slot(h, d, 0)
            w_wait(h, slot)
            w_send(h, slot, h, other, part)
    for d in (back, ahead):
        for h in (0, 1):
            for e in (ahead, back):
                w_send(h, me.slot(h, d, 0), 1 - h, e)
    compute(0, 0)
    for h in (0, 1):
        slot = me.slot(h, 2, 0)
        w_wait(h, slot, 0)
        w_wait(h, slot, 1)
        for e in (ahead, back):
            w_send(h, slot, 1 - h, e)

    def pass_on(du):
        for d, other, part in ((back, ahead, 0), (ahead, back, 1)):
            for h in (0, 1):
                slot = me.slot(h, du, d)
                w_wait(h, slot)
                w_send(h, slot, 1 - h, other, part)

    pass_on(0)

    @pl.loop(0, 4)
    def _(i):
        a, b = lax.div(i, 2), lax.rem(i, 2)
        compute((1 - a) * (1 + 2 * b), a * (1 + 2 * b))

    pass_on(back)
    pass_on(ahead)

    @pl.loop(0, 4)
    def _(i):
        a, b = lax.div(i, 2), lax.rem(i, 2)
        compute(1 + 2 * a, 1 + 2 * b)

    pass_on(2)

    def far(du):
        for h in (0, 1):
            for part in (0, 1):
                w_wait(h, me.slot(h, du, 2), part)

    far(0)

    @pl.loop(0, 2)
    def _(i):
        compute(2 * i, 2 * (1 - i))

    far(back)
    far(ahead)

    @pl.loop(0, 4)
    def _(i):
        a, b = lax.div(i, 2), lax.rem(i, 2)
        compute((1 - a) * 2 + a * (1 + 2 * b), a * 2 + (1 - a) * (1 + 2 * b))

    far(2)
    compute(2, 2)

    def kv_block(ctx):
        return pl.ds(ctx * 2, 2)

    pout[...] = acc[rows:, :]
    send(pout, pin, p_sem.at[0], me.partner())

    @pl.loop(0, 2 * heads)
    def _(i):
        for copy in q_copies(i):
            copy.start()

    arrived(pin, p_sem.at[0], me)
    kv_ref[kv_block(me.ctx)] = (acc[:rows, :] + pin[...]).astype(BF).reshape(2, STRETCH, 2 * hd)

    def block(d):
        return lax.rem(me.z + d, DEPTH) * 2 + me.core

    half = rows // 2

    def z_part(d, part):
        return kv_ref.at[block(d) * 2 + part]

    def z_send(d, step, part):
        ref, sem = z_part(d, part), z_sem.at[block(d), part]
        send(ref, ref, sem, me.along_z(step))

    def z_wait(d, part):
        arrived(z_part(d, part), z_sem.at[block(d), part], me)

    def share(d):
        ref = kv_ref.at[kv_block(block(d))]
        send(ref, ref, c_sem.at[block(d)], me.partner())

    up, down = 1, DEPTH - 1
    for first in (0, 1):
        z_send(0, up, first)
        z_send(0, down, 1 - first)
    share(0)

    n_stretch = order_ref.shape[0]

    @pl.loop(0, n_stretch)
    def _(i):
        at = jnp.int32(0)
        for b in range(n_stretch):
            at = jnp.where(order_ref[b] == i, b, at)
        where_ref[i] = at

    for k in (1, 2, 3):
        for first in (0, 1):
            z_wait(DEPTH - k, first)
            if k < 3 or first == 0:
                z_send(DEPTH - k, up, first)
            z_wait(k, 1 - first)
            if k < 3 or first == 0:
                z_send(k, down, 1 - first)
        if k == 3:
            for d, step, part in ((DEPTH - 3, up, 0), (3, down, 1)):
                ref = z_part(d, part)
                send(ref, ref, e_sem.at[part], me.across(step))
        share(DEPTH - k)
        share(k)
    z_wait(4, 0)
    z_wait(4, 1)
    for d in range(DEPTH):
        other = lax.rem(me.z + d, DEPTH) * 2 + 1 - me.core
        if d == 4:
            for part in (0, 1):
                arrived(kv_ref.at[other * 2 + part], e_sem.at[part], me)
        else:
            arrived(kv_ref.at[kv_block(other)], c_sem.at[other], me)

    factor = math.log2(math.e) / math.sqrt(hd)
    scale = 1.0 / math.sqrt(hd)
    width = heads * STRETCH
    nt = (((1,), (1,)), ((), ()))

    def first_of(t):
        return jnp.maximum(order_ref[me.ctx * 2 + t] - (SPAN - 1), 0)

    @pl.loop(0, 2 * heads)
    def _(i):
        for copy in q_copies(i):
            copy.wait()

    for t in (0, 1):
        for at in (0, SPAN + 1):
            sums[t, at] = jnp.zeros((STRETCH, 2 * hd), F32)
    inner = slice(1, SPAN + 1)

    @pl.loop(0, 2)
    def _(t):
        place, first = order_ref[me.ctx * 2 + t], first_of(t)

        @pl.loop(0, SPAN)
        def _(i):
            kw[pl.ds(pl.multiple_of(i * STRETCH, STRETCH), STRETCH)] = kv_ref[where_ref[first + i]]

        spot = place * STRETCH + lax.rem(lax.broadcasted_iota(jnp.int32, (1, width), 1), STRETCH)
        low = jnp.zeros_like(spot)
        end = jnp.int32(0)
        for d in range(lens_ref.shape[0]):
            end = end + lens_ref[d]
            low = jnp.where(spot >= end, end, low)
        low, high = low - first * STRETCH, spot - first * STRETCH
        at = lax.broadcasted_iota(jnp.int32, (SPAN * STRETCH, width), 0)
        s = lax.dot_general(kw[:, :hd], qs[t], nt, preferred_element_type=F32)
        s = jnp.where((at >= low) & (at <= high), s, -1e30)
        scores[...] = s
        top = jnp.max(s, axis=0, keepdims=True)
        dprobs[...] = lax.dot_general(kw[:, hd:], gs[t], nt, preferred_element_type=F32)
        e = jnp.exp2((scores[...] - top) * factor)
        scores[...] = e
        inverse = 1.0 / jnp.sum(e, axis=0, keepdims=True)
        delta = jnp.sum(e * dprobs[...], axis=0, keepdims=True) * inverse
        p = scores[...] * inverse
        ds = (p * (dprobs[...] - delta)).astype(BF)
        sums[t, inner, :, :hd] = jnp.dot(ds, qs[t], preferred_element_type=F32).reshape(SPAN, STRETCH, hd)
        sums[t, inner, :, hd:] = jnp.dot(p.astype(BF), gs[t], preferred_element_type=F32).reshape(SPAN, STRETCH, hd)
        dqt = lax.dot_general(kw[:, :hd], ds, (((0,), (0,)), ((), ())), preferred_element_type=F32)
        dq = (jnp.transpose(dqt) * scale).astype(BF)
        row = pl.ds(pl.multiple_of(t * STRETCH, STRETCH), STRETCH)
        for h in range(heads):
            dqs[row, h * hd : (h + 1) * hd] = dq[h * STRETCH : (h + 1) * STRETCH]

    dq_copy = pltpu.make_async_copy(dqs, dq_ref, dq_sem.at[0])
    dq_copy.start()

    def stretch_grads(b):
        total = jnp.zeros((STRETCH, 2 * hd), F32)
        for t in (0, 1):
            i = jnp.minimum(jnp.maximum(order_ref[b] - first_of(t) + 1, 0), SPAN + 1)
            total = total + sums[t, i]
        return jnp.concatenate([total[:, :hd] * scale, total[:, hd:]], axis=1)

    z_steps = (1, DEPTH - 1)

    def z_at(d):
        return lax.rem(me.z + d, DEPTH)

    def target(w, k):
        return 4 - k if w == 0 else DEPTH - 4 + k

    pieces = (pl.ds(0, STRETCH), pl.ds(STRETCH, STRETCH))

    def stretch(d, core, piece):
        return (z_at(d) * 2 + core) * 2 + piece

    for d in (4, 3, 5, 2, 6, 1, 7, 0):
        for piece in (0, 1):
            rout[d, pieces[piece]] = stretch_grads(stretch(d, 1 - me.core, piece)).astype(BF)
        send(rout.at[d], rbuf.at[d], d1_sem.at[d], me.partner())

    known = set()

    def own_sum(d, piece):
        if d not in known:
            known.add(d)
            arrived(rbuf.at[d], d1_sem.at[d], me)
        return stretch_grads(stretch(d, me.core, piece)) + rbuf[d, pieces[piece]].astype(F32)

    def kv_step(w, k, piece, first):
        total = own_sum(target(w, k), piece)
        if not first:
            arrived(zin.at[w, k - 1, pieces[piece]], d2_sem.at[w, k - 1, piece], me)
            total = total + zin[w, k - 1, pieces[piece]].astype(F32)
        ref = zout.at[w, k, pieces[piece]]
        ref[...] = total.astype(BF)
        send(ref, zin.at[w, k, pieces[piece]], d2_sem.at[w, k, piece], me.along_z(z_steps[w]))

    for w in (0, 1):
        kv_step(w, 0, w, True)
    for w in (0, 1):
        kv_step(w, 1, 1 - w, True)
    for k in (1, 2, 3):
        for w in (0, 1):
            kv_step(w, k, w, False)
        if k < 3:
            for w in (0, 1):
                kv_step(w, k + 1, 1 - w, False)
    for piece in (0, 1):
        total = own_sum(0, piece)
        for w in (0, 1):
            arrived(zin.at[w, 3, pieces[piece]], d2_sem.at[w, 3, piece], me)
            total = total + zin[w, 3, pieces[piece]].astype(F32)
        ref = gbuf.at[0, pieces[piece]]
        ref[...] = total.astype(BF)
        send(ref, gbuf.at[1, pieces[piece]], d3_sem.at[piece], me.partner())
    gt[:, :rows] = jnp.transpose(gbuf[0].astype(F32)).astype(BF)

    for piece in (0, 1):
        arrived(gbuf.at[1, pieces[piece]], d3_sem.at[piece], me)
    gt[:, rows:] = jnp.transpose(gbuf[1].astype(F32)).astype(BF)

    groups = DEPTH // 2

    def terms(dx, dy):
        s = slot_of(me.x + dx, me.y + dy)
        t = jnp.dot(gt[...], hbuf[s], preferred_element_type=F32).astype(BF)
        for j in range(DEPTH):
            h, g = divmod(j, groups)
            tb[j, s] = t[h * hd : (h + 1) * hd, g * hd : (g + 1) * hd]

    sides = (1, SIDE - 1)

    def flat(h, slot, dv, w=None):
        cut = 48 if dv % 2 == 0 else 32
        at = pl.ds(0, FLAT_ROWS) if w is None else pl.ds(0, cut) if w == 0 else pl.ds(cut, FLAT_ROWS - cut)
        return tb.at[pl.ds(groups * h, groups), slot, at], at

    def first_sends(h):
        for dv in (2, 1, 3, 0):
            for w in (0, 1):
                ref, at = flat(h, me.slot(h, 2, dv), dv, w)
                send(ref, pr0.at[h, w, dv, :, at], p0_sem.at[h, w, dv], me.along(h, sides[w]))

    @pl.loop(0, SIDE)
    def _(i):
        terms(2, i)

    first_sends(0)

    @pl.loop(0, SIDE - 1)
    def _(i):
        terms(i + lax.div(i, 2), 2)

    first_sends(1)

    @pl.loop(0, (SIDE - 1) * (SIDE - 1))
    def _(i):
        a, b = lax.div(i, 3), lax.rem(i, 3)
        terms(a + lax.div(a, 2), b + lax.div(b, 2))

    def add(ref, *got):
        total = ref[...].astype(F32)
        for g in got:
            total = total + g.astype(F32)
        ref[...] = total.astype(BF)

    deep = pl.ds(FLAT_ROWS, hd - FLAT_ROWS)
    slots = (pl.ds(0, n // 2), pl.ds(n // 2, n // 2))

    def deep_step(k, w, piece, first=False):
        ref = tb.at[z_at(target(w, k)), slots[piece], deep]
        if not first:
            got = cin.at[w, k - 1, slots[piece]]
            arrived(got, n_sem.at[w, k - 1, piece], me)
            add(ref, got[...])
        send(ref, cin.at[w, k, slots[piece]], n_sem.at[w, k, piece], me.along_z(z_steps[w]))

    def second_sends(dv):
        for h in (0, 1):
            for w in (0, 1):
                slot = me.slot(h, sides[w], dv)
                ref, at = flat(h, slot, dv, w)
                got = pr0.at[h, w, dv, :, at]
                arrived(got, p0_sem.at[h, w, dv], me)
                add(ref, got[...])
                send(flat(h, slot, dv)[0], pr1.at[h, w, dv], p1_sem.at[h, w, dv], me.along(h, sides[w]))

    def collect(h, dv):
        for w in (0, 1):
            arrived(pr1.at[h, w, dv], p1_sem.at[h, w, dv], me)
        add(flat(h, me.slot(h, 0, dv), dv)[0], pr1[h, 0, dv], pr1[h, 1, dv])

    def third_sends(h):
        for w in (0, 1):
            ref, at = flat(h, me.slot(h, 0, 2), h, w)
            send(ref, qr0.at[h, w, :, at], q0_sem.at[h, w], me.along(1 - h, sides[w]))

    def fourth_sends(h, w):
        slot = me.slot(h, 0, sides[w])
        ref, at = flat(h, slot, h, w)
        got = qr0.at[h, w, :, at]
        arrived(got, q0_sem.at[h, w], me)
        add(ref, got[...])
        send(flat(h, slot, 0)[0], qr1.at[h, w], q1_sem.at[h, w], me.along(1 - h, sides[w]))

    for w in (0, 1):
        deep_step(0, w, w, True)
    for w in (0, 1):
        deep_step(1, w, 1 - w, True)
    second_sends(2)
    second_sends(1)
    for w in (0, 1):
        deep_step(1, w, w)
    second_sends(3)
    second_sends(0)
    for w in (0, 1):
        deep_step(2, w, 1 - w)
    for h in (0, 1):
        collect(h, 2)
        third_sends(h)
    for w in (0, 1):
        deep_step(2, w, w)
    for w in (0, 1):
        for h in (0, 1):
            collect(h, sides[w])
            fourth_sends(h, w)
    for w in (0, 1):
        deep_step(3, w, 1 - w)
    for h in (0, 1):
        collect(h, 0)
    for w in (0, 1):
        deep_step(3, w, w)
    for h in (0, 1):
        for w in (0, 1):
            arrived(qr1.at[h, w], q1_sem.at[h, w], me)
        add(flat(h, me.dp, 0)[0], qr1[h, 0], qr1[h, 1])
    rows_first = pl.ds(0, FLAT_ROWS)
    for d in (4, 3, 5, 2, 6, 1, 7):
        send(tb.at[z_at(d), me.dp, rows_first], zr.at[d], f_sem.at[d], me.along_z(d))
    for piece in (0, 1):
        ref = tb.at[me.z, slots[piece], deep]
        for w in (0, 1):
            arrived(cin.at[w, 3, slots[piece]], n_sem.at[w, 3, piece], me)
        add(ref, cin[0, 3, slots[piece]], cin[1, 3, slots[piece]])
    for far in range(4, 0, -1):
        for dx in range(SIDE):
            for dy in range(SIDE):
                if min(dx, SIDE - dx) + min(dy, SIDE - dy) == far:
                    slot = slot_of(me.x + dx, me.y + dy)
                    send(tb.at[me.z, slot, deep], xr.at[dy * SIDE + dx], x_sem.at[dy * SIDE + dx], (slot, me.ctx))

    top = tb[me.z, me.dp, rows_first].astype(F32)
    for d in range(1, DEPTH):
        arrived(zr.at[d], f_sem.at[d], me)
        top = top + zr[d].astype(F32)
    low = tb[me.z, me.dp, deep].astype(F32)
    for i in range(1, n):
        arrived(xr.at[i], x_sem.at[i], me)
        low = low + xr[i].astype(F32)
    done = jnp.transpose(jnp.concatenate([top, low], axis=0)).astype(BF)

    def block(d, core):
        j = z_at(d)
        at = core * cols + lax.rem(j, groups) * hd
        return out_ref.at[lax.div(j, groups), pl.ds(pl.multiple_of(at, hd), hd)]

    def share_block(d):
        send(block(d, me.core), block(d, me.core), b_sem.at[d], me.partner())

    block(0, me.core)[...] = done
    for d in (4, 3, 5, 2, 6, 1, 7):
        send(block(0, me.core), block(0, me.core), g_sem.at[d], me.along_z(d))
    share_block(0)
    for d in (1, 7, 2, 6, 3, 5, 4):
        arrived(block(d, me.core), g_sem.at[DEPTH - d], me)
        share_block(d)
    for d in range(DEPTH):
        arrived(block(d, 1 - me.core), b_sem.at[d], me)
    send.finish()
    dq_copy.wait()

    @pl.loop(0, n)
    def _(s):
        h_copies(s)[1].wait_send()


def finish_kernel(dq_ref, sums_ref, dq_out, key_out, value_out):
    dq_out[...] = dq_ref[...]
    key_out[...] = sums_ref[0].astype(F32)
    value_out[...] = sums_ref[1].astype(F32)


def finish(query_grad, sums):
    steps = 2
    (rows, width), (_, depth, hd) = query_grad.shape, sums.shape
    dq_spec = pl.BlockSpec((rows // steps, width), lambda i: (i, 0))
    out_spec = pl.BlockSpec((depth // steps, hd), lambda i: (i, 0))
    return pl.pallas_call(
        finish_kernel,
        grid=(steps,),
        out_shape=(
            jax.ShapeDtypeStruct(query_grad.shape, BF),
            jax.ShapeDtypeStruct((depth, hd), F32),
            jax.ShapeDtypeStruct((depth, hd), F32),
        ),
        in_specs=[dq_spec, pl.BlockSpec((2, depth // steps, hd), lambda i: (0, i, 0))],
        out_specs=(dq_spec, out_spec, out_spec),
        name="finish",
    )(query_grad, sums)


def on_device(hidden_in, queries, grad_out, w_key, w_value, stretch_order, doc_lengths):
    hidden = hidden_in[0]
    rows, hd = hidden.shape[0], w_key.shape[1]
    n = SIDE * SIDE
    cols = hidden.shape[1] // n // 2
    width, span = 2 * hd, SPAN * STRETCH
    heads = queries.shape[2] // hd
    groups = DEPTH // 2
    dma = pltpu.SemaphoreType.DMA
    smem, hbm = pl.BlockSpec(memory_space=pltpu.SMEM), pl.BlockSpec(memory_space=pl.ANY)
    query_grad, sums = pl.pallas_call(
        kernel,
        out_shape=(
            jax.ShapeDtypeStruct((rows, heads * hd), BF),
            jax.ShapeDtypeStruct((2, 2 * cols, hd), BF),
        ),
        in_specs=[hbm] * 5 + [smem] * 2,
        out_specs=(hbm, pl.BlockSpec(memory_space=pltpu.VMEM)),
        scratch_shapes=[
            pltpu.VMEM((n, 2 * rows, cols), BF),
            pltpu.VMEM((2, n, cols, hd), BF),
            pltpu.VMEM((2 * rows, width), F32),
            pltpu.VMEM((rows, width), F32),
            pltpu.VMEM((rows, width), F32),
            pltpu.VMEM((2 * 2 * DEPTH, STRETCH, width), BF),
            pltpu.SMEM(stretch_order.shape, jnp.int32),
            pltpu.VMEM((2, heads * STRETCH, hd), BF),
            pltpu.VMEM((2, heads * STRETCH, hd), BF),
            pltpu.VMEM((span, width), BF),
            pltpu.VMEM((span, heads * STRETCH), F32),
            pltpu.VMEM((span, heads * STRETCH), F32),
            pltpu.VMEM((2, SPAN + 2, STRETCH, width), F32),
            pltpu.VMEM((rows, heads * hd), BF),
            pltpu.VMEM((DEPTH, n, hd, hd), BF),
            pltpu.VMEM((DEPTH, rows, width), BF),
            pltpu.VMEM((DEPTH, rows, width), BF),
            pltpu.VMEM((2, 4, rows, width), BF),
            pltpu.VMEM((2, 4, rows, width), BF),
            pltpu.VMEM((2, rows, width), BF),
            pltpu.VMEM((width, 2 * rows), BF),
            pltpu.VMEM((2, 2, SIDE, groups, FLAT_ROWS, hd), BF),
            pltpu.VMEM((2, 2, SIDE, groups, FLAT_ROWS, hd), BF),
            pltpu.VMEM((2, 2, groups, FLAT_ROWS, hd), BF),
            pltpu.VMEM((2, 2, groups, FLAT_ROWS, hd), BF),
            pltpu.VMEM((2, 4, n, hd - FLAT_ROWS, hd), BF),
            pltpu.VMEM((DEPTH, FLAT_ROWS, hd), BF),
            pltpu.VMEM((n, hd - FLAT_ROWS, hd), BF),
            dma((SENDS,)),
            dma((n,)),
            dma((n,)),
            dma((n,)),
            dma((2,)),
            dma((2 * heads,)),
            dma((2 * heads,)),
            dma((1,)),
            dma((2, n, 2)),
            dma((1,)),
            dma((2 * DEPTH, 2)),
            dma((2 * DEPTH,)),
            dma((2,)),
            dma((DEPTH,)),
            dma((2, 4, 2)),
            dma((2,)),
            dma((2, 2, SIDE)),
            dma((2, 2, SIDE)),
            dma((2, 2)),
            dma((2, 2)),
            dma((2, 4, 2)),
            dma((DEPTH,)),
            dma((n,)),
            dma((DEPTH,)),
            dma((DEPTH,)),
        ],
        compiler_params=pltpu.CompilerParams(
            collective_id=0, has_side_effects=True, vmem_limit_bytes=VMEM_LIMIT
        ),
        name="kv_backward",
    )(hidden, queries[0], grad_out[0], w_key, w_value, stretch_order, doc_lengths[0])
    query_grad, key_sums, value_sums = finish(query_grad, sums)
    return query_grad[None], key_sums, value_sums


def solution(mesh):
    return jax.shard_map(
        on_device,
        mesh=mesh,
        in_specs=(
            P("dp", "ctx", None),
            P("dp", "ctx", None),
            P("dp", "ctx", None),
            P("dp", None),
            P("dp", None),
            P(),
            P("dp", None),
        ),
        out_specs=(P("dp", "ctx", None), P("dp", None), P("dp", None)),
        check_vma=False,
    )
```
